32 devices in a mesh: seq: 8 (over z, y), dp: 4 (over x, core).
Axes of the slice: x: 2, y: 2, z: 4, core: 2. Of those that a mesh axis runs over, the one named last changes fastest.
Arguments:
- layer_rows: bfloat16 [4, 1024, 1024], P('dp', 'seq'), may hold values from -6 to 6
- doc_ids: int32 [4, 1024], P('dp', 'seq'), may hold values from 0 to 5, never falling along the last dimension, each value on 1 to 512 neighbouring positions
- packing: int32 [4, 8], P('dp'), may hold values from 0 to 7, each once within a row
- norm_gain: float32 [1024], replicated, may hold values from 0.1 to 1.9
- w_qkv: bfloat16 [1024, 3072], replicated, may hold values from -0.1875 to 0.1875
- d_attn: bfloat16 [4, 1024, 1024], P('dp', 'seq'), may hold values from -6 to 6
Outputs:
- d_input: bfloat16 [4, 1024, 1024], P('dp', 'seq')
- w_grad: float32 [1024, 3072], P('seq')
The draws below stay inside these ranges and needn't reach their ends.
Inputs may be any that keep to these rules, and one draw needn't show every extreme that they name: `doc_ids`: in each group the song numbers never fall along the initial order; every number occurs, and one song spans exactly 512 frames. `packing`: each group's row names every block number once.
All inputs are finite; a program needn't handle non-finite values.
Results may differ from the reference program's by a relative error of at most 0.024.
Values may be sent and summed in bfloat16 or wider, within the bound.
A program may use at most 128 MiB of HBM per device.

```python
import math
import jax
import jax.numpy as jnp
import numpy as np
from jax import lax

D = 1024
HEADS = 8
HEAD = 128
TOK_DEV = 128
BLOCK = 128
DOCS = 6
HD = 1024
SEQ_LEN = 1024
GROUPS = 4
NBLK = 8
ALL_TOKENS = 4096
N_SEQ = 8


def steps_of(own_key, extent, cuts, least, high):
    def one(position, blocks):
        heights = jax.random.uniform(jax.random.fold_in(jax.random.fold_in(own_key, 6), position), (blocks,), jnp.float32, least / len(cuts), high / len(cuts))
        return jnp.repeat(jnp.exp(heights), extent[position] // blocks).reshape((-1,) + (1,) * (len(extent) - position - 1))

    loudness = one(*cuts[0])
    for cut in cuts[1:]:
        loudness = loudness * one(*cut)
    return loudness


def profile(number_of, total, reach, skew):
    weights = [(1 << 20) // math.isqrt(rank ** skew) + 1 for rank in range(2, number_of + 1)]
    surplus, counts = total - reach - (number_of - 1), [1] * (number_of - 1)
    while surplus > 0:
        free = [i for i in range(number_of - 1) if counts[i] < reach]
        whole, left = sum([weights[i] for i in free]), surplus
        for i in free:
            extra = min(reach - counts[i], max(1, left * weights[i] // whole), surplus)
            counts[i] = counts[i] + extra
            surplus = surplus - extra
    return np.array([reach] + counts)


def uneven(key, count, total, reach, lean):
    if count == 2:
        one = jax.random.randint(key, (), max(1, total - reach), min(reach, total - 1) + 1)
        return jnp.stack([one, total - one])
    lengths = jnp.asarray(profile(count, total, reach, lean), jnp.int32)
    pairs = (count - 1) // 2
    source_of, receiver = lengths[1:1 + 2 * pairs:2], lengths[2:2 + 2 * pairs:2]
    margin = jnp.minimum(source_of - 1, reach - receiver)
    moved = jax.random.randint(jax.random.fold_in(key, 1), (pairs,), 0, 1 << 20) % (margin + 1)
    lengths = lengths.at[1:1 + 2 * pairs:2].set(source_of - moved).at[2:2 + 2 * pairs:2].set(receiver + moved)
    return lengths[jax.random.permutation(jax.random.fold_in(key, 2), count)]


def centred(stream_key, extent, scale, bound, shards=(), kind=jnp.bfloat16):
    loudness = steps_of(stream_key, extent, shards, -0.22, 0.18) if shards else 1.0
    drawn = jax.random.normal(stream_key, extent, jnp.float32) * scale * loudness
    return jnp.minimum(jnp.maximum(drawn, -bound), bound).astype(kind)


def setup_inputs(seed: int = 0) -> dict:
    keys = jax.random.split(jax.random.key(seed), 7)
    return {
        "layer_rows": centred(keys[0], (GROUPS, SEQ_LEN, D), 1.0, 6.0, ((0, 4), (1, 8))),
        "doc_ids": jax.vmap(lambda own: jnp.searchsorted(jnp.cumsum(uneven(own, DOCS, SEQ_LEN, SEQ_LEN // 2, 2)), jnp.arange(SEQ_LEN), side="right"))(jax.random.split(keys[1], GROUPS)).reshape((GROUPS, SEQ_LEN)).astype(jnp.int32),
        "packing": jax.vmap(lambda own: jax.random.permutation(own, NBLK))(jax.random.split(keys[2], GROUPS)).reshape((GROUPS, NBLK)).astype(jnp.int32),
        "norm_gain": jnp.clip(1.0 + 0.18 * jax.random.normal(keys[3], (D,), jnp.float32), 0.1, 1.9),
        "w_qkv": centred(keys[4], (D, 3 * HD), D ** -0.5, 0.1875),
        "d_attn": centred(keys[5], (GROUPS, SEQ_LEN, HD), 1.0, 6.0, ((0, 4), (1, 8))),
    }


def rounded(value):
    return lax.optimization_barrier(value.astype(jnp.bfloat16)).astype(jnp.float32)

def normalize(frames, norm_gain):
    values = frames.astype(jnp.float32)
    inverse = lax.rsqrt(lax.optimization_barrier(jnp.mean(values * values, axis=-1, keepdims=True)) + 1e-05)
    unit_rows = values * inverse
    return (inverse, unit_rows, (unit_rows * norm_gain).astype(jnp.bfloat16))

def shard_grads(queries, grad_out, query_docs, query_pos, all_keys, all_values, key_docs, key_pos):
    head_cols = HEADS * HEAD
    factor = 1.0 / math.sqrt(HEAD)
    q_heads = queries.astype(jnp.float32).reshape(-1, HEADS, HEAD)
    k_heads = all_keys.astype(jnp.float32).reshape(-1, HEADS, HEAD)
    v_heads = all_values.astype(jnp.float32).reshape(-1, HEADS, HEAD)
    g_heads = grad_out.astype(jnp.float32).reshape(-1, HEADS, HEAD)
    allowed = (query_docs[:, None] == key_docs[None, :]) & (key_pos[None, :] <= query_pos[:, None])
    scores = jnp.einsum('qhd,khd->hqk', q_heads, k_heads) * factor
    expon = jnp.where(allowed[None], jnp.exp(scores), jnp.float32(0.0))
    attn_prob = expon / lax.optimization_barrier(jnp.sum(expon, axis=-1, keepdims=True))
    prob_low = rounded(attn_prob)
    outputs = jnp.einsum('hqk,khd->qhd', prob_low, v_heads)
    row_delta = lax.optimization_barrier(jnp.sum(g_heads * outputs, axis=-1))
    grad_prob = jnp.einsum('qhd,khd->hqk', g_heads, v_heads)
    dscore = rounded(attn_prob * (grad_prob - row_delta.T[:, :, None]))
    dquery = jnp.einsum('hqk,khd->qhd', dscore, k_heads) * factor
    dkey = jnp.einsum('hqk,qhd->khd', dscore, q_heads) * factor
    dvalue = jnp.einsum('hqk,qhd->khd', prob_low, g_heads)
    key_part = jnp.concatenate([dkey.reshape(-1, head_cols), dvalue.reshape(-1, head_cols)], axis=1)
    return (dquery.reshape(-1, head_cols), rounded(key_part))

def reference(layer_rows, doc_ids, packing, norm_gain, w_qkv, d_attn):
    head_cols = HEADS * HEAD
    shard_ids = jnp.arange(N_SEQ, dtype=jnp.int32)

    def group_grads(w_sum, inputs):
        rows_group, doc_group, pack_group, grad_group = inputs
        packed = rows_group.reshape(NBLK, BLOCK, D)[pack_group].reshape(SEQ_LEN, D)
        packed_docs = doc_group.reshape(NBLK, BLOCK)[pack_group].reshape(SEQ_LEN)
        positions = (pack_group[:, None] * BLOCK + jnp.arange(BLOCK, dtype=jnp.int32)[None, :]).reshape(SEQ_LEN)
        inverse, unit_rows, normed = normalize(packed, norm_gain)
        projected = jnp.dot(normed, w_qkv, preferred_element_type=jnp.float32).astype(jnp.bfloat16)
        queries = projected[:, :head_cols]
        all_keys = projected[:, head_cols:2 * head_cols]
        all_values = projected[:, 2 * head_cols:]

        def per_shard(key_sum, shard_idx):
            first_row = (shard_idx * TOK_DEV).astype(jnp.int32)
            dquery, key_part = shard_grads(lax.dynamic_slice_in_dim(queries, first_row, TOK_DEV, 0), lax.dynamic_slice_in_dim(grad_group, first_row, TOK_DEV, 0), lax.dynamic_slice_in_dim(packed_docs, first_row, TOK_DEV, 0), lax.dynamic_slice_in_dim(positions, first_row, TOK_DEV, 0), all_keys, all_values, packed_docs, positions)
            return (key_sum + key_part, dquery)
        key_sum, dquery = lax.scan(per_shard, jnp.zeros((SEQ_LEN, 2 * head_cols), jnp.float32), shard_ids)
        grad_qkv = jnp.concatenate([dquery.reshape(SEQ_LEN, head_cols), key_sum], axis=1).astype(jnp.bfloat16)
        d_normed = jnp.dot(grad_qkv, w_qkv.T, preferred_element_type=jnp.float32)
        gained = d_normed * norm_gain
        d_frames = (inverse * (gained - unit_rows * lax.optimization_barrier(jnp.mean(gained * unit_rows, axis=-1, keepdims=True)))).astype(jnp.bfloat16)

        def weight_part(total, shard_idx):
            first_row = (shard_idx * TOK_DEV).astype(jnp.int32)
            normed_run = lax.dynamic_slice_in_dim(normed, first_row, TOK_DEV, 0)
            grads_run = lax.dynamic_slice_in_dim(grad_qkv, first_row, TOK_DEV, 0)
            return (total + rounded(jnp.dot(normed_run.T, grads_run, preferred_element_type=jnp.float32)), jnp.float32(0.0))
        w_sum, ignored = lax.scan(weight_part, w_sum, shard_ids)
        return (w_sum, d_frames)
    w_sum, d_input = lax.scan(group_grads, jnp.zeros((D, 3 * head_cols), jnp.float32), (layer_rows, doc_ids, packing, d_attn))
    w_grad = w_sum * (1.0 / math.sqrt(ALL_TOKENS))
    return (d_input, w_grad)
```

```python
import functools
import math

import jax
import jax.numpy as jnp
from jax import lax
from jax.experimental import pallas as pl
from jax.experimental.pallas import tpu as pltpu
from jax.sharding import PartitionSpec as P

HEADS = 8
HEAD = 128
BLOCK = 128
DOCS = 6
EPS = 1e-05
FACTOR = 1.0 / math.sqrt(HEAD)
MESH = pl.DeviceIdType.MESH
VMEM_LIMIT = 56 * 1024 * 1024
NT = (((1,), (1,)), ((), ()))
TN = (((0,), (0,)), ((), ()))


def remote(src, dst, send, recv, **where):
    return pltpu.make_async_remote_copy(
        src_ref=src, dst_ref=dst, send_sem=send, recv_sem=recv, device_id=where, device_id_type=MESH
    )


def gather_kernel(
    n, frames, grads, docs, all_frames, head_grads, all_docs,
    own_sem, zs, zr, ys, yr, gs, gr, ds, dr,
):
    me = lax.axis_index("seq")
    partner = me + 1 - 2 * lax.rem(me, 2)
    half = n // 2
    peers = [lax.rem(me + k, n) for k in range(1, n)]

    def head_of(device):
        start = pl.multiple_of(lax.rem(device, HEADS) * HEAD, HEAD)
        return grads.at[:, pl.ds(start, HEAD)]

    barrier = pltpu.get_barrier_semaphore()
    for peer in peers:
        pl.semaphore_signal(barrier, inc=1, device_id={"seq": peer}, device_id_type=MESH)
    own = [
        pltpu.make_async_copy(frames, all_frames.at[me], own_sem.at[0]),
        pltpu.make_async_copy(head_of(me), head_grads.at[me], own_sem.at[1]),
        pltpu.make_async_copy(docs, all_docs.at[me], own_sem.at[2]),
    ]
    for copy in own:
        copy.start()
    pl.semaphore_wait(barrier, n - 1)

    column = [
        remote(frames, all_frames.at[me], zs.at[k - 1], zr.at[k - 1], seq=lax.rem(me + 2 * k, n))
        for k in range(1, half)
    ]
    across = [remote(frames, all_frames.at[me], ys.at[0], yr.at[0], seq=partner)]
    for copy in column + across:
        copy.start()
    rest = []
    for k in range(1, n):
        rest.append(remote(docs, all_docs.at[me], ds.at[k - 1], dr.at[k - 1], seq=peers[k - 1]))
        rest.append(
            remote(head_of(peers[k - 1]), head_grads.at[me], gs.at[k - 1], gr.at[k - 1], seq=peers[k - 1])
        )
    for copy in rest:
        copy.start()
    for k in range(1, half):
        column[k - 1].wait_recv()
        block = lax.rem(me - 2 * k + n, n)
        forward = remote(all_frames.at[block], all_frames.at[block], ys.at[k], yr.at[k], seq=partner)
        forward.start()
        across.append(forward)
    for copy in own:
        copy.wait()
    for copy in column:
        copy.wait_send()
    for copy in across + rest:
        copy.wait()


def gather(n, frames, grads, docs):
    rows, width = frames.shape
    dma = pltpu.SemaphoreType.DMA
    any_spec = pl.BlockSpec(memory_space=pl.ANY)
    return pl.pallas_call(
        functools.partial(gather_kernel, n),
        out_shape=(
            jax.ShapeDtypeStruct((n, rows, width), jnp.bfloat16),
            jax.ShapeDtypeStruct((n, rows, HEAD), jnp.bfloat16),
            jax.ShapeDtypeStruct((n, 1, rows), jnp.int32),
        ),
        in_specs=[any_spec] * 3,
        out_specs=(any_spec,) * 3,
        scratch_shapes=[
            dma((3,)), dma((n // 2,)), dma((n // 2,)), dma((n // 2,)), dma((n // 2,)),
            dma((n,)), dma((n,)), dma((n,)), dma((n,)),
        ],
        compiler_params=pltpu.CompilerParams(collective_id=0, has_side_effects=True),
        name="gather",
    )(frames, grads, docs)


def normalized(frames, gain):
    values = frames.astype(jnp.float32)
    inverse = lax.rsqrt(jnp.mean(values * values, axis=-1, keepdims=True) + EPS)
    unit = values * inverse
    return inverse, unit, (unit * gain).astype(jnp.bfloat16)


def head_kernel(
    n, packing, head, frames, gain, wq, wk, wv, docs, grads, g_out, w_out,
    normed_s, q_s, k_s, v_s, g_s, pos_s, dk_s, dv_s,
):
    step = pl.program_id(0)
    rows = pl.ds(pl.multiple_of(step * BLOCK, BLOCK), BLOCK)
    normed = normalized(frames[0], gain[...])[2]
    normed_s[rows, :] = normed
    for weight, kept in ((wq, q_s), (wk, k_s), (wv, v_s)):
        kept[rows, :] = jnp.dot(normed, weight[...], preferred_element_type=jnp.float32).astype(
            jnp.bfloat16
        )
    pos_s[rows, :] = packing[step] * BLOCK + lax.broadcasted_iota(jnp.int32, (BLOCK, BLOCK), 0)

    @pl.when(step == n - 1)
    def attention():
        numbers = docs[...]
        lane = lax.broadcasted_iota(jnp.int32, (1, BLOCK), 1)
        counts = [
            jnp.sum((numbers == d).astype(jnp.float32)).astype(jnp.int32) for d in range(DOCS - 1)
        ]
        dk_s[...] = jnp.zeros_like(dk_s)
        dv_s[...] = jnp.zeros_like(dv_s)

        def first_of(block):
            own = docs[block]
            start = jnp.zeros_like(own)
            for d in range(DOCS - 1):
                start = start + jnp.where(own > d, counts[d], 0)
            return start

        def queries(i, carry):
            low, high = packing[2 * i], packing[2 * i + 1]
            first = jnp.concatenate([first_of(low), first_of(high)], axis=1)
            last = jnp.concatenate([low * BLOCK + lane, high * BLOCK + lane], axis=1)
            here = pl.ds(pl.multiple_of(i * 2 * BLOCK, 2 * BLOCK), 2 * BLOCK)
            q = q_s[here, :]
            g = grads[pl.ds(2 * i, 2)].reshape(2 * BLOCK, HEAD)
            pos = jnp.concatenate([pos_s[...], pos_s[...]], axis=1)
            scores = lax.dot_general(k_s[...], q, NT, preferred_element_type=jnp.float32)
            expon = jnp.where(
                (pos >= first) & (pos <= last),
                jnp.exp2(scores * (FACTOR * math.log2(math.e))),
                0.0,
            )
            prob = expon * (1.0 / jnp.sum(expon, axis=0, keepdims=True))
            prob_low = prob.astype(jnp.bfloat16)
            grad_prob = lax.dot_general(v_s[...], g, NT, preferred_element_type=jnp.float32)
            delta = jnp.sum(prob_low.astype(jnp.float32) * grad_prob, axis=0, keepdims=True)
            dscore = (prob * (grad_prob - delta)).astype(jnp.bfloat16)
            dk_s[...] += jnp.dot(dscore, q, preferred_element_type=jnp.float32)
            dv_s[...] += jnp.dot(prob_low, g, preferred_element_type=jnp.float32)
            dq = lax.dot_general(dscore, k_s[...], TN, preferred_element_type=jnp.float32)
            g_s[here, :HEAD] = (dq * FACTOR).astype(jnp.bfloat16)
            return carry

        lax.fori_loop(0, n // 2, queries, 0)
        g_s[:, HEAD : 2 * HEAD] = (dk_s[...] * FACTOR).astype(jnp.bfloat16)
        g_s[:, 2 * HEAD :] = dv_s[...].astype(jnp.bfloat16)
        g_out[...] = g_s[...].reshape(g_out.shape)
        w_out[...] = (
            lax.dot_general(normed_s[...], g_s[...], TN, preferred_element_type=jnp.float32)
            .astype(jnp.bfloat16)
            .reshape(w_out.shape)
        )


def head_grads_of(n, packing, head, all_frames, gain, w_qkv, all_docs, head_grads):
    width = all_frames.shape[2]
    total = n * BLOCK

    def weight(j):
        return pl.BlockSpec((width, HEAD), lambda r, packing, head: (0, j * HEADS + head[0]))

    def whole(shape):
        return pl.BlockSpec(shape, lambda r, packing, head: (0,) * len(shape))

    return pl.pallas_call(
        functools.partial(head_kernel, n),
        grid_spec=pltpu.PrefetchScalarGridSpec(
            num_scalar_prefetch=2,
            grid=(n,),
            in_specs=[
                pl.BlockSpec((1, BLOCK, width), lambda r, packing, head: (packing[r], 0, 0)),
                whole((1, width)),
                weight(0), weight(1), weight(2),
                whole((n, 1, BLOCK)),
                whole((n, BLOCK, HEAD)),
            ],
            out_specs=(whole((n, BLOCK, 3 * HEAD)), whole((n, width // n, 3 * HEAD))),
            scratch_shapes=[
                pltpu.VMEM((total, width), jnp.bfloat16),
                pltpu.VMEM((total, HEAD), jnp.bfloat16),
                pltpu.VMEM((total, HEAD), jnp.bfloat16),
                pltpu.VMEM((total, HEAD), jnp.bfloat16),
                pltpu.VMEM((total, 3 * HEAD), jnp.bfloat16),
                pltpu.VMEM((total, BLOCK), jnp.int32),
                pltpu.VMEM((total, HEAD), jnp.float32),
                pltpu.VMEM((total, HEAD), jnp.float32),
            ],
        ),
        out_shape=(
            jax.ShapeDtypeStruct((n, BLOCK, 3 * HEAD), jnp.bfloat16),
            jax.ShapeDtypeStruct((n, width // n, 3 * HEAD), jnp.bfloat16),
        ),
        compiler_params=pltpu.CompilerParams(vmem_limit_bytes=VMEM_LIMIT),
        name="head_grads",
    )(packing, head, all_frames, gain, w_qkv, w_qkv, w_qkv, all_docs, head_grads)


def halvings(rows, groups):
    sizes = []
    for _ in range(groups.bit_length() - 1):
        halved = rows % 32 == 0
        rows = rows // 2 if halved else rows
        sizes.append((rows, halved))
    return sizes


def exchange_kernel(n, groups, g_in, w_in, g_all, w_all, *scratch):
    sizes = halvings(w_in.shape[1], groups)
    count = len(sizes)
    landed, sums = scratch[:count], scratch[count : 2 * count]
    own_sem, gs, gr, ws, wr, ps, pr, bs, br = scratch[2 * count :]
    me = lax.axis_index("seq")
    dp = lax.axis_index("dp")
    peers = [lax.rem(me + k, n) for k in range(1, n)]
    bits = [lax.rem(dp // (1 << b), 2) for b in range(count)]
    partners = [dp + (1 << b) * (1 - 2 * bits[b]) for b in range(count)]

    barrier = pltpu.get_barrier_semaphore()
    for peer in peers:
        pl.semaphore_signal(barrier, inc=1, device_id={"seq": peer}, device_id_type=MESH)
    for partner in partners:
        pl.semaphore_signal(barrier, inc=1, device_id={"dp": partner}, device_id_type=MESH)
    own_g = pltpu.make_async_copy(g_in.at[me], g_all.at[me], own_sem.at[0])
    own_g.start()
    pl.semaphore_wait(barrier, n - 1 + count)

    held, offset, waits = w_in, 0, []
    for b, (size, halved) in enumerate(sizes):
        other = pl.multiple_of((1 - bits[b]) * size, size) if halved else 0
        mine = pl.multiple_of(bits[b] * size, size) if halved else 0
        send = remote(
            held.at[:, pl.ds(other, size), :], landed[b], ws.at[b], wr.at[b], dp=partners[b]
        )
        send.start()
        if b == 0:
            for k in range(1, n):
                copy = remote(
                    g_in.at[peers[k - 1]], g_all.at[me], gs.at[k - 1], gr.at[k - 1], seq=peers[k - 1]
                )
                copy.start()
                waits.append(copy)
        send.wait_recv()
        sums[b][...] = (
            held[:, pl.ds(mine, size), :].astype(jnp.float32) + landed[b][...].astype(jnp.float32)
        ).astype(jnp.bfloat16)
        send.wait_send()
        held, offset = sums[b], offset + mine
    size = sizes[-1][0]
    here = pl.ds(pl.multiple_of(offset, size), size)
    own_w = pltpu.make_async_copy(held.at[me], w_all.at[me, here, :], own_sem.at[1])
    own_w.start()
    parts = []
    for k in range(1, n):
        copy = remote(
            held.at[peers[k - 1]], w_all.at[me, here, :], ps.at[k - 1], pr.at[k - 1], seq=peers[k - 1]
        )
        copy.start()
        parts.append(copy)
    own_w.wait()
    for copy in parts:
        copy.wait()
    for b in reversed(range(count)):
        size, halved = sizes[b]
        if halved:
            here = pl.ds(pl.multiple_of(offset, size), size)
            copy = remote(
                w_all.at[:, here, :], w_all.at[:, here, :], bs.at[b], br.at[b], dp=partners[b]
            )
            copy.start()
            copy.wait()
            offset = offset - bits[b] * size
    own_g.wait()
    for copy in waits:
        copy.wait()


def exchange(n, groups, g_in, w_in):
    rows = w_in.shape[1]
    dma = pltpu.SemaphoreType.DMA
    sizes = halvings(rows, groups)
    count = len(sizes)
    any_spec = pl.BlockSpec(memory_space=pl.ANY)
    buffers = [pltpu.VMEM((n, size, 3 * HEAD), jnp.bfloat16) for size, _ in sizes]
    return pl.pallas_call(
        functools.partial(exchange_kernel, n, groups),
        out_shape=(
            jax.ShapeDtypeStruct(g_in.shape, jnp.bfloat16),
            jax.ShapeDtypeStruct(w_in.shape, jnp.bfloat16),
        ),
        in_specs=[any_spec, pl.BlockSpec(memory_space=pltpu.VMEM)],
        out_specs=(any_spec, any_spec),
        scratch_shapes=buffers + buffers + [
            dma((2,)), dma((n,)), dma((n,)), dma((count,)), dma((count,)),
            dma((n,)), dma((n,)), dma((count,)), dma((count,)),
        ],
        compiler_params=pltpu.CompilerParams(
            collective_id=1, has_side_effects=True, vmem_limit_bytes=VMEM_LIMIT
        ),
        name="exchange",
    )(g_in, w_in)


def finish_kernel(scale, packing, head, frames, gain, g_all, w_all, w_qkv, d_out, w_out, total):
    j = pl.program_id(0)
    columns = jnp.concatenate([g_all[h] for h in range(HEADS)], axis=1)
    part = lax.dot_general(columns, w_qkv[...], NT, preferred_element_type=jnp.float32)
    for h in range(HEADS):
        w_out[:, h * HEAD : (h + 1) * HEAD] = w_all[h].astype(jnp.float32) * scale

    @pl.when(j == 0)
    def first():
        total[...] = part

    @pl.when(j > 0)
    def later():
        total[...] += part

    @pl.when(j == 2)
    def last():
        inverse, unit, _ = normalized(frames[0], gain[...])
        gained = total[...] * gain[...]
        mean = jnp.mean(gained * unit, axis=-1, keepdims=True)
        d_out[...] = (inverse * (gained - unit * mean)).astype(jnp.bfloat16)


def finish(n, scale, packing, index, all_frames, gain, w_qkv, g_all, w_all):
    width = all_frames.shape[2]
    rows = w_all.shape[1]
    return pl.pallas_call(
        functools.partial(finish_kernel, scale),
        grid_spec=pltpu.PrefetchScalarGridSpec(
            num_scalar_prefetch=2,
            grid=(3,),
            in_specs=[
                pl.BlockSpec((1, BLOCK, width), lambda j, packing, index: (packing[index[0]], 0, 0)),
                pl.BlockSpec((1, width), lambda j, packing, index: (0, 0)),
                pl.BlockSpec((n, BLOCK, HEAD), lambda j, packing, index: (0, 0, j)),
                pl.BlockSpec((n, rows, HEAD), lambda j, packing, index: (0, 0, j)),
                pl.BlockSpec((width, HEADS * HEAD), lambda j, packing, index: (0, j)),
            ],
            out_specs=(
                pl.BlockSpec((BLOCK, width), lambda j, packing, index: (0, 0)),
                pl.BlockSpec((rows, HEADS * HEAD), lambda j, packing, index: (0, j)),
            ),
            scratch_shapes=[pltpu.VMEM((BLOCK, width), jnp.float32)],
        ),
        out_shape=(
            jax.ShapeDtypeStruct((BLOCK, width), jnp.bfloat16),
            jax.ShapeDtypeStruct((rows, 3 * HEADS * HEAD), jnp.float32),
        ),
        compiler_params=pltpu.CompilerParams(vmem_limit_bytes=VMEM_LIMIT),
        name="finish",
    )(packing, index, all_frames, gain, g_all, w_all, w_qkv)


def body(n, groups, layer_rows, doc_ids, packing, norm_gain, w_qkv, d_attn):
    index = lax.axis_index("seq").astype(jnp.int32).reshape(1)
    order = packing[0]
    gain = norm_gain.reshape(1, -1)
    all_frames, head_grads, all_docs = gather(n, layer_rows[0], d_attn[0], doc_ids)
    g_in, w_in = head_grads_of(
        n, order, lax.rem(index, HEADS), all_frames, gain, w_qkv, all_docs, head_grads
    )
    g_all, w_all = exchange(n, groups, g_in, w_in)
    scale = 1.0 / math.sqrt(n * BLOCK * groups)
    d_frames, w_grad = finish(n, scale, order, index, all_frames, gain, w_qkv, g_all, w_all)
    return d_frames[None], w_grad


def solution(mesh):
    return jax.shard_map(
        functools.partial(body, mesh.shape["seq"], mesh.shape["dp"]),
        mesh=mesh,
        in_specs=(
            P("dp", "seq", None),
            P("dp", "seq"),
            P("dp", None),
            P(),
            P(),
            P("dp", "seq", None),
        ),
        out_specs=(P("dp", "seq", None), P("seq", None)),
        check_vma=False,
    )
```

```python
import functools
import math

import jax
import jax.numpy as jnp
from jax import lax
from jax.experimental import pallas as pl
from jax.experimental.pallas import tpu as pltpu
from jax.sharding import PartitionSpec as P

HEADS = 8
HEAD = 128
BLOCK = 128
DOCS = 6
EPS = 1e-05
FACTOR = 1.0 / math.sqrt(HEAD)
MESH = pl.DeviceIdType.MESH
VMEM_LIMIT = 56 * 1024 * 1024
CHUNKS = 2
NT = (((1,), (1,)), ((), ()))
TN = (((0,), (0,)), ((), ()))


def remote(src, dst, send, recv, **where):
    return pltpu.make_async_remote_copy(
        src_ref=src, dst_ref=dst, send_sem=send, recv_sem=recv, device_id=where, device_id_type=MESH
    )


def normalized(frames, gain):
    values = frames.astype(jnp.float32)
    inverse = lax.rsqrt(jnp.mean(values * values, axis=-1, keepdims=True) + EPS)
    unit = values * inverse
    return inverse, unit, (unit * gain).astype(jnp.bfloat16)


def halvings(rows, groups):
    sizes = []
    for _ in range(groups.bit_length() - 1):
        halved = rows % 32 == 0
        rows = rows // 2 if halved else rows
        sizes.append((rows, halved))
    return sizes


def kernel(
    n, groups, scale, chosen, frames, gain, w_qkv, docs, grads, d_out, w_out,
    frames_s, docs_s, grads_s, weights_s, normed_s, q_s, k_s, v_s, dk_s, dv_s,
    g_s, g_send, g_all, w_part, w_all, own_sem, *scratch,
):
    sizes = halvings(w_part.shape[1], groups)
    count = len(sizes)
    landed, sums = scratch[:count], scratch[count : 2 * count]
    zs, zr, ys, yr, ds, dr, ts, tr, gs, gr, ws, wr, ps, pr, bs, br = scratch[2 * count :]
    me = lax.axis_index("seq")
    dp = lax.axis_index("dp")
    side = lax.rem(me, 2)
    place = me // 2
    partner = me + 1 - 2 * side
    length = n // 2
    part = BLOCK // CHUNKS
    head = lax.rem(me, HEADS)
    peers = [lax.rem(me + k, n) for k in range(1, n)]
    bits = [lax.rem(dp // (1 << b), 2) for b in range(count)]
    partners = [dp + (1 << b) * (1 - 2 * bits[b]) for b in range(count)]

    def head_of(device):
        start = pl.multiple_of(lax.rem(device, HEADS) * HEAD, HEAD)
        return grads.at[:, pl.ds(start, HEAD)]

    barrier = pltpu.get_barrier_semaphore()
    for peer in peers:
        pl.semaphore_signal(barrier, inc=1, device_id={"seq": peer}, device_id_type=MESH)
    for other in partners:
        pl.semaphore_signal(barrier, inc=1, device_id={"dp": other}, device_id_type=MESH)
    own_frames = pltpu.make_async_copy(frames, frames_s.at[me], own_sem.at[0])
    own_weights = pltpu.make_async_copy(w_qkv, weights_s, own_sem.at[1])
    own_grads = pltpu.make_async_copy(head_of(me), grads_s.at[me], own_sem.at[2])
    own_docs = pltpu.make_async_copy(docs, docs_s.at[me], own_sem.at[3])
    for copy in (own_frames, own_weights, own_grads, own_docs):
        copy.start()
    pl.semaphore_wait(barrier, n - 1 + count)

    def piece(block, chunk):
        return frames_s.at[block, pl.ds(chunk * part, part), :]

    def along(way, hop, chunk, block, source=None):
        return remote(
            piece(block, chunk) if source is None else source, piece(block, chunk),
            zs.at[way, hop, chunk], zr.at[way, hop, chunk], seq=me + (2 if way == 0 else -2),
        )

    def across(way, hop, chunk, block, source=None):
        return remote(
            piece(block, chunk) if source is None else source, piece(block, chunk),
            ys.at[way, hop, chunk], yr.at[way, hop, chunk], seq=partner,
        )

    def can_send(way, hop):
        if way == 0:
            return (place + 1 < length) & (place - hop >= 0)
        return (place - 1 >= 0) & (place + hop < length)

    def arrives(way, hop):
        return place - 1 - hop >= 0 if way == 0 else place + 1 + hop < length

    def origin(way, hop):
        return me - 2 * (hop + 1) if way == 0 else me + 2 * (hop + 1)

    for chunk in range(CHUNKS):
        source = frames.at[pl.ds(chunk * part, part), :]
        for way in range(2):
            @pl.when(can_send(way, 0))
            def _():
                along(way, 0, chunk, me, source).start()
        across(0, 0, chunk, me, source).start()
    small = []
    for k in range(1, n):
        small.append(remote(docs, docs_s.at[me], ds.at[k - 1], dr.at[k - 1], seq=peers[k - 1]))
        small.append(
            remote(head_of(peers[k - 1]), grads_s.at[me], ts.at[k - 1], tr.at[k - 1], seq=peers[k - 1])
        )
    for copy in small:
        copy.start()

    def project(block):
        rows = pl.ds(pl.multiple_of(block * BLOCK, BLOCK), BLOCK)
        normed = normalized(frames_s[block], gain[...])[2]
        normed_s[rows, :] = normed
        for j, kept in enumerate((q_s, k_s, v_s)):
            columns = pl.ds(pl.multiple_of((j * HEADS + head) * HEAD, HEAD), HEAD)
            kept[rows, :] = jnp.dot(
                normed, weights_s[:, columns], preferred_element_type=jnp.float32
            ).astype(jnp.bfloat16)

    own_frames.wait()
    own_weights.wait()
    project(me)
    for hop in range(length - 1):
        for chunk in range(CHUNKS):
            for way in range(2):
                @pl.when(arrives(way, hop))
                def _():
                    block = origin(way, hop)
                    along(way, hop, chunk, block).wait_recv()
                    if hop + 1 < length - 1:
                        @pl.when(can_send(way, hop + 1))
                        def _():
                            along(way, hop + 1, chunk, block).start()
                    across(way, hop + 1, chunk, block).start()
        for way in range(2):
            @pl.when(arrives(way, hop))
            def _():
                project(origin(way, hop))
            if hop == 0 and way == 0:
                for chunk in range(CHUNKS):
                    across(0, 0, chunk, partner).wait_recv()
                project(partner)
            if hop > 0:
                @pl.when(arrives(way, hop - 1))
                def _():
                    block = origin(way, hop - 1) + partner - me
                    for chunk in range(CHUNKS):
                        across(way, hop, chunk, block).wait_recv()
                    project(block)
    for way in range(2):
        @pl.when(arrives(way, length - 2))
        def _():
            block = origin(way, length - 2) + partner - me
            for chunk in range(CHUNKS):
                across(way, length - 1, chunk, block).wait_recv()
            project(block)
    own_grads.wait()
    own_docs.wait()
    for copy in small:
        copy.wait()

    numbers = docs_s[...]
    counts = [
        jnp.sum(
            jnp.sum(jnp.where(numbers == d, 1.0, 0.0), axis=0), axis=-1, keepdims=True
        )
        for d in range(DOCS - 1)
    ]

    def first_of(block):
        own = docs_s[block]
        start = jnp.zeros(own.shape, jnp.float32)
        for d in range(DOCS - 1):
            start = start + jnp.where(own > d, counts[d], 0.0)
        return start.astype(jnp.int32)

    def pick(weight_of, block_of, width):
        total = None
        for b in range(n):
            weight = jnp.concatenate([weight_of(b).astype(jnp.bfloat16)] * (width // HEAD), axis=1)
            term = weight * block_of(b)
            total = term if total is None else total + term
        return total

    def grads_of(block):
        return pick(lambda r: chosen[r * n + block], lambda r: grads_s[r], HEAD)

    dk_s[...] = jnp.zeros_like(dk_s)
    dv_s[...] = jnp.zeros_like(dv_s)
    for i in range(n // 2):
        low, high = 2 * i * BLOCK, 2 * (i + 1) * BLOCK
        first = jnp.concatenate([first_of(2 * i), first_of(2 * i + 1)], axis=1)
        last = low + lax.broadcasted_iota(jnp.int32, (1, 2 * BLOCK), 1)
        pos = lax.broadcasted_iota(jnp.int32, (high, 2 * BLOCK), 0)
        q = q_s[low:high, :]
        g = jnp.concatenate([grads_of(2 * i), grads_of(2 * i + 1)], axis=0)
        keys = k_s[:high, :]
        scores = lax.dot_general(keys, q, NT, preferred_element_type=jnp.float32)
        expon = jnp.where(
            (pos >= first) & (pos <= last),
            jnp.exp2(scores * (FACTOR * math.log2(math.e))),
            0.0,
        )
        prob = expon * (1.0 / jnp.sum(expon, axis=0, keepdims=True))
        prob_low = prob.astype(jnp.bfloat16)
        grad_prob = lax.dot_general(v_s[:high, :], g, NT, preferred_element_type=jnp.float32)
        delta = jnp.sum(prob_low.astype(jnp.float32) * grad_prob, axis=0, keepdims=True)
        dscore = (prob * (grad_prob - delta)).astype(jnp.bfloat16)
        dk_s[:high, :] += jnp.dot(dscore, q, preferred_element_type=jnp.float32)
        dv_s[:high, :] += jnp.dot(prob_low, g, preferred_element_type=jnp.float32)
        dq = lax.dot_general(dscore, keys, TN, preferred_element_type=jnp.float32)
        g_s[low:high, :HEAD] = (dq * FACTOR).astype(jnp.bfloat16)
    g_s[:, HEAD : 2 * HEAD] = (dk_s[...] * FACTOR).astype(jnp.bfloat16)
    g_s[:, 2 * HEAD :] = dv_s[...].astype(jnp.bfloat16)

    def stage(r, carry):
        g_send[r] = pick(
            lambda b: chosen[r * n + b], lambda b: g_s[b * BLOCK : (b + 1) * BLOCK, :], 3 * HEAD
        )
        return carry

    lax.fori_loop(0, n, stage, 0)
    own_g = pltpu.make_async_copy(g_send.at[me], g_all.at[me], own_sem.at[4])
    own_g.start()
    sent_g = []
    for k in range(1, n):
        copy = remote(
            g_send.at[peers[k - 1]], g_all.at[me], gs.at[k - 1], gr.at[k - 1], seq=peers[k - 1]
        )
        copy.start()
        sent_g.append(copy)

    w_part[...] = (
        lax.dot_general(normed_s[...], g_s[...], TN, preferred_element_type=jnp.float32)
        .astype(jnp.bfloat16)
        .reshape(w_part.shape)
    )
    held, offset = w_part, 0
    for b, (size, halved) in enumerate(sizes):
        other = pl.multiple_of((1 - bits[b]) * size, size) if halved else 0
        mine = pl.multiple_of(bits[b] * size, size) if halved else 0
        send = remote(
            held.at[:, pl.ds(other, size), :], landed[b], ws.at[b], wr.at[b], dp=partners[b]
        )
        send.start()
        send.wait_recv()
        sums[b][...] = (
            held[:, pl.ds(mine, size), :].astype(jnp.float32) + landed[b][...].astype(jnp.float32)
        ).astype(jnp.bfloat16)
        send.wait_send()
        held, offset = sums[b], offset + mine
    size = sizes[-1][0]
    here = pl.ds(pl.multiple_of(offset, size), size)
    own_w = pltpu.make_async_copy(held.at[me], w_all.at[me, here, :], own_sem.at[5])
    own_w.start()
    sent_w = []
    for k in range(1, n):
        copy = remote(
            held.at[peers[k - 1]], w_all.at[me, here, :], ps.at[k - 1], pr.at[k - 1], seq=peers[k - 1]
        )
        copy.start()
        sent_w.append(copy)

    own_g.wait()
    for copy in sent_g:
        copy.wait()

    def d_input():
        total = jnp.zeros(d_out.shape, jnp.float32)
        for j in range(3):
            columns = jnp.concatenate(
                [g_all[h, :, j * HEAD : (j + 1) * HEAD] for h in range(HEADS)], axis=1
            )
            total = total + lax.dot_general(
                columns, weights_s[:, j * HEADS * HEAD : (j + 1) * HEADS * HEAD], NT,
                preferred_element_type=jnp.float32,
            )
        inverse, unit, _ = normalized(
            pick(lambda b: chosen[me * n + b], lambda b: frames_s[b], frames_s.shape[2]), gain[...]
        )
        gained = total * gain[...]
        mean = jnp.mean(gained * unit, axis=-1, keepdims=True)
        d_out[...] = (inverse * (gained - unit * mean)).astype(jnp.bfloat16)

    own_w.wait()
    for copy in sent_w:
        copy.wait()
    done = False
    for b in reversed(range(count)):
        size, halved = sizes[b]
        if halved:
            here = pl.ds(pl.multiple_of(offset, size), size)
            copy = remote(
                w_all.at[:, here, :], w_all.at[:, here, :], bs.at[b], br.at[b], dp=partners[b]
            )
            copy.start()
            if not done:
                d_input()
                done = True
            copy.wait()
            offset = offset - bits[b] * size
    if not done:
        d_input()
    for h in range(HEADS):
        for j in range(3):
            start = (j * HEADS + h) * HEAD
            w_out[:, start : start + HEAD] = (
                w_all[h, :, j * HEAD : (j + 1) * HEAD].astype(jnp.float32) * scale
            )

    for chunk in range(CHUNKS):
        across(0, 0, chunk, me).wait_send()
        for way in range(2):
            for hop in range(length - 1):
                @pl.when(can_send(way, hop))
                def _():
                    along(way, hop, chunk, me).wait_send()

                @pl.when(arrives(way, hop))
                def _():
                    across(way, hop + 1, chunk, me).wait_send()


def body(n, groups, layer_rows, doc_ids, packing, norm_gain, w_qkv, d_attn):
    width = w_qkv.shape[0]
    total = n * BLOCK
    rows = width // n
    sizes = halvings(rows, groups)
    count = len(sizes)
    dma = pltpu.SemaphoreType.DMA
    low = jnp.bfloat16
    chosen = jnp.broadcast_to(
        (packing[0][:, None] == jnp.arange(n)[None, :]).astype(jnp.float32).reshape(n * n, 1, 1),
        (n * n, 1, HEAD),
    )
    hbm = pl.BlockSpec(memory_space=pl.ANY)
    vmem = pl.BlockSpec(memory_space=pltpu.VMEM)
    buffers = [pltpu.VMEM((n, size, 3 * HEAD), low) for size, _ in sizes]
    routes = dma((2, n // 2, CHUNKS))
    d_frames, w_grad = pl.pallas_call(
        functools.partial(kernel, n, groups, 1.0 / math.sqrt(total * groups)),
        out_shape=(
            jax.ShapeDtypeStruct((BLOCK, width), low),
            jax.ShapeDtypeStruct((rows, 3 * HEADS * HEAD), jnp.float32),
        ),
        in_specs=[vmem, hbm, vmem, hbm, hbm, hbm],
        out_specs=(vmem, vmem),
        scratch_shapes=[
            pltpu.VMEM((n, BLOCK, width), low),
            pltpu.VMEM((n, 1, BLOCK), jnp.int32),
            pltpu.VMEM((n, BLOCK, HEAD), low),
            pltpu.VMEM(w_qkv.shape, low),
            pltpu.VMEM((total, width), low),
            pltpu.VMEM((total, HEAD), low),
            pltpu.VMEM((total, HEAD), low),
            pltpu.VMEM((total, HEAD), low),
            pltpu.VMEM((total, HEAD), jnp.float32),
            pltpu.VMEM((total, HEAD), jnp.float32),
            pltpu.VMEM((total, 3 * HEAD), low),
            pltpu.VMEM((n, BLOCK, 3 * HEAD), low),
            pltpu.VMEM((n, BLOCK, 3 * HEAD), low),
            pltpu.VMEM((n, rows, 3 * HEAD), low),
            pltpu.VMEM((n, rows, 3 * HEAD), low),
            dma((6,)),
            *buffers, *buffers,
            routes, routes, routes, routes,
            dma((n,)), dma((n,)), dma((n,)), dma((n,)), dma((n,)), dma((n,)),
            dma((count,)), dma((count,)), dma((n,)), dma((n,)), dma((count,)), dma((count,)),
        ],
        compiler_params=pltpu.CompilerParams(
            collective_id=0, has_side_effects=True, vmem_limit_bytes=VMEM_LIMIT
        ),
        name="attention_backward",
    )(chosen, layer_rows[0], norm_gain.reshape(1, -1), w_qkv, doc_ids, d_attn[0])
    return d_frames[None], w_grad


def solution(mesh):
    return jax.shard_map(
        functools.partial(body, mesh.shape["seq"], mesh.shape["dp"]),
        mesh=mesh,
        in_specs=(
            P("dp", "seq", None),
            P("dp", "seq"),
            P("dp", None),
            P(),
            P(),
            P("dp", "seq", None),
        ),
        out_specs=(P("dp", "seq", None), P("seq", None)),
        check_vma=False,
    )
```

```python
import functools
import math

import jax
import jax.numpy as jnp
from jax import lax
from jax.experimental import pallas as pl
from jax.experimental.pallas import tpu as pltpu
from jax.sharding import PartitionSpec as P

HEADS = 8
HEAD = 128
BLOCK = 128
DOCS = 6
EPS = 1e-05
FACTOR = 1.0 / math.sqrt(HEAD)
MESH = pl.DeviceIdType.MESH
VMEM_LIMIT = 56 * 1024 * 1024
CHUNKS = 4
NT = (((1,), (1,)), ((), ()))
TN = (((0,), (0,)), ((), ()))


def remote(src, dst, send, recv, **where):
    return pltpu.make_async_remote_copy(
        src_ref=src, dst_ref=dst, send_sem=send, recv_sem=recv, device_id=where, device_id_type=MESH
    )


def normalized(frames, gain):
    values = frames.astype(jnp.float32)
    inverse = lax.rsqrt(jnp.mean(values * values, axis=-1, keepdims=True) + EPS)
    unit = values * inverse
    return inverse, unit, (unit * gain).astype(jnp.bfloat16)


def halvings(rows, groups):
    sizes = []
    for _ in range(groups.bit_length() - 1):
        halved = rows % 32 == 0
        rows = rows // 2 if halved else rows
        sizes.append((rows, halved))
    return sizes


def kernel(
    n, groups, packing, frames, gain, w_qkv, docs, grads, d_out, w_all,
    frames_s, docs_s, grads_s, weights_s, normed_s, q_s, k_s, v_s, dk_s, dv_s,
    g_s, g_send, g_all, w_part, chosen, d_s, own_sem, *scratch,
):
    sizes = halvings(w_part.shape[1], groups)
    count = len(sizes)
    landed, sums = scratch[:count], scratch[count : 2 * count]
    zs, zr, ys, yr, ds, dr, ts, tr, gs, gr, hs, hr, ws, wr, ps, pr, bs, br = scratch[2 * count :]
    me = lax.axis_index("seq")
    dp = lax.axis_index("dp")
    side = lax.rem(me, 2)
    place = me // 2
    partner = me + 1 - 2 * side
    length = n // 2
    part = BLOCK // CHUNKS
    head = lax.rem(me, HEADS)
    peers = [lax.rem(me + k, n) for k in range(1, n)]
    bits = [lax.rem(dp // (1 << b), 2) for b in range(count)]
    partners = [dp + (1 << b) * (1 - 2 * bits[b]) for b in range(count)]

    def head_of(device):
        start = pl.multiple_of(lax.rem(device, HEADS) * HEAD, HEAD)
        return grads.at[:, pl.ds(start, HEAD)]

    barrier = pltpu.get_barrier_semaphore()
    for peer in peers:
        pl.semaphore_signal(barrier, inc=1, device_id={"seq": peer}, device_id_type=MESH)
    for other in partners:
        pl.semaphore_signal(barrier, inc=1, device_id={"dp": other}, device_id_type=MESH)
    own_frames = pltpu.make_async_copy(frames, frames_s.at[me], own_sem.at[0])
    own_weights = pltpu.make_async_copy(w_qkv, weights_s, own_sem.at[1])
    own_grads = pltpu.make_async_copy(head_of(me), grads_s.at[me], own_sem.at[2])
    own_docs = pltpu.make_async_copy(docs, docs_s.at[me], own_sem.at[3])
    for copy in (own_frames, own_weights, own_grads, own_docs):
        copy.start()
    pl.semaphore_wait(barrier, n - 1 + count)

    def piece(block, chunk):
        return frames_s.at[block, pl.ds(chunk * part, part), :]

    def along(way, hop, chunk, block, source=None):
        return remote(
            piece(block, chunk) if source is None else source, piece(block, chunk),
            zs.at[way, hop, chunk], zr.at[way, hop, chunk], seq=me + (2 if way == 0 else -2),
        )

    def across(way, hop, chunk, block, source=None):
        return remote(
            piece(block, chunk) if source is None else source, piece(block, chunk),
            ys.at[way, hop, chunk], yr.at[way, hop, chunk], seq=partner,
        )

    def can_send(way, hop):
        if way == 0:
            return (place + 1 < length) & (place - hop >= 0)
        return (place - 1 >= 0) & (place + hop < length)

    def arrives(way, hop):
        return place - 1 - hop >= 0 if way == 0 else place + 1 + hop < length

    def origin(way, hop):
        return me - 2 * (hop + 1) if way == 0 else me + 2 * (hop + 1)

    for chunk in range(CHUNKS):
        source = frames.at[pl.ds(chunk * part, part), :]
        for way in range(2):
            @pl.when(can_send(way, 0))
            def _():
                along(way, 0, chunk, me, source).start()
        across(0, 0, chunk, me, source).start()
    small = []
    for k in range(1, n):
        small.append(remote(docs, docs_s.at[me], ds.at[k - 1], dr.at[k - 1], seq=peers[k - 1]))
        small.append(
            remote(head_of(peers[k - 1]), grads_s.at[me], ts.at[k - 1], tr.at[k - 1], seq=peers[k - 1])
        )
    for copy in small:
        copy.start()

    def project(block):
        rows = pl.ds(pl.multiple_of(block * BLOCK, BLOCK), BLOCK)
        normed = normalized(frames_s[block], gain[...])[2]
        normed_s[rows, :] = normed
        for j, kept in enumerate((q_s, k_s, v_s)):
            columns = pl.ds(pl.multiple_of((j * HEADS + head) * HEAD, HEAD), HEAD)
            kept[rows, :] = jnp.dot(
                normed, weights_s[:, columns], preferred_element_type=jnp.float32
            ).astype(jnp.bfloat16)

    order = packing[...]
    for r in range(n):
        for b in range(n):
            chosen[r * n + b] = jnp.broadcast_to(
                jnp.where(order[:, r : r + 1] == b, 1.0, 0.0), (1, HEAD)
            )
    own_frames.wait()
    own_weights.wait()
    project(me)
    for hop in range(length - 1):
        for chunk in range(CHUNKS):
            for way in range(2):
                @pl.when(arrives(way, hop))
                def _():
                    block = origin(way, hop)
                    along(way, hop, chunk, block).wait_recv()
                    if hop + 1 < length - 1:
                        @pl.when(can_send(way, hop + 1))
                        def _():
                            along(way, hop + 1, chunk, block).start()
                    across(way, hop + 1, chunk, block).start()
        for way in range(2):
            @pl.when(arrives(way, hop))
            def _():
                project(origin(way, hop))
        if hop == 0:
            for chunk in range(CHUNKS):
                across(0, 0, chunk, partner).wait_recv()
            project(partner)
    for hop in range(1, length):
        for way in range(2):
            @pl.when(arrives(way, hop - 1))
            def _():
                block = origin(way, hop - 1) + partner - me
                for chunk in range(CHUNKS):
                    across(way, hop, chunk, block).wait_recv()
                project(block)
    own_grads.wait()
    own_docs.wait()
    for copy in small:
        copy.wait()

    numbers = docs_s[...]
    counts = [
        jnp.sum(
            jnp.sum(jnp.where(numbers == d, 1.0, 0.0), axis=0), axis=-1, keepdims=True
        )
        for d in range(DOCS - 1)
    ]

    def first_of(block):
        own = docs_s[block]
        start = jnp.zeros(own.shape, jnp.float32)
        for d in range(DOCS - 1):
            start = start + jnp.where(own > d, counts[d], 0.0)
        return start.astype(jnp.int32)

    def pick(weight_of, block_of, width):
        total = None
        for b in range(n):
            weight = jnp.concatenate([weight_of(b).astype(jnp.bfloat16)] * (width // HEAD), axis=1)
            term = weight * block_of(b)
            total = term if total is None else total + term
        return total

    def grads_of(block):
        return pick(lambda r: chosen[r * n + block], lambda r: grads_s[r], HEAD)

    dk_s[...] = jnp.zeros_like(dk_s)
    dv_s[...] = jnp.zeros_like(dv_s)
    for i in range(n // 2):
        low, high = 2 * i * BLOCK, 2 * (i + 1) * BLOCK
        first = jnp.concatenate([first_of(2 * i), first_of(2 * i + 1)], axis=1)
        last = low + lax.broadcasted_iota(jnp.int32, (1, 2 * BLOCK), 1)
        pos = lax.broadcasted_iota(jnp.int32, (high, 2 * BLOCK), 0)
        q = q_s[low:high, :]
        g = jnp.concatenate([grads_of(2 * i), grads_of(2 * i + 1)], axis=0)
        keys = k_s[:high, :]
        scores = lax.dot_general(keys, q, NT, preferred_element_type=jnp.float32)
        expon = jnp.where(
            (pos >= first) & (pos <= last),
            jnp.exp2(scores * (FACTOR * math.log2(math.e))),
            0.0,
        )
        prob = expon * (1.0 / jnp.sum(expon, axis=0, keepdims=True))
        prob_low = prob.astype(jnp.bfloat16)
        grad_prob = lax.dot_general(v_s[:high, :], g, NT, preferred_element_type=jnp.float32)
        delta = jnp.sum(prob_low.astype(jnp.float32) * grad_prob, axis=0, keepdims=True)
        dscore = (prob * (grad_prob - delta)).astype(jnp.bfloat16)
        dk_s[:high, :] += jnp.dot(dscore, q, preferred_element_type=jnp.float32)
        dv_s[:high, :] += jnp.dot(prob_low, g, preferred_element_type=jnp.float32)
        dq = lax.dot_general(dscore, keys, TN, preferred_element_type=jnp.float32)
        g_s[low:high, :HEAD] = (dq * FACTOR).astype(jnp.bfloat16)
    g_s[:, HEAD : 2 * HEAD] = (dk_s[...] * FACTOR).astype(jnp.bfloat16)
    g_s[:, 2 * HEAD :] = dv_s[...].astype(jnp.bfloat16)

    def stage(r, carry):
        g_send[r] = pick(
            lambda b: chosen[r * n + b], lambda b: g_s[b * BLOCK : (b + 1) * BLOCK, :], 3 * HEAD
        )
        return carry

    lax.fori_loop(0, n, stage, 0)
    own_g = pltpu.make_async_copy(g_send.at[me], g_all.at[me], own_sem.at[4])
    own_g.start()
    sent_g = []
    sent_v = []
    qk, vv = pl.ds(0, 2 * HEAD), pl.ds(2 * HEAD, HEAD)
    for k in range(1, n):
        peer = peers[k - 1]
        sent_g.append(
            remote(g_send.at[peer, :, qk], g_all.at[me, :, qk], gs.at[k - 1], gr.at[k - 1], seq=peer)
        )
        sent_v.append(
            remote(g_send.at[peer, :, vv], g_all.at[me, :, vv], hs.at[k - 1], hr.at[k - 1], seq=peer)
        )
    for copy in sent_g:
        copy.start()

    w_part[...] = (
        lax.dot_general(normed_s[...], g_s[...], TN, preferred_element_type=jnp.float32)
        .astype(jnp.bfloat16)
        .reshape(w_part.shape)
    )
    held, offset = w_part, 0
    for b, (size, halved) in enumerate(sizes):
        other = pl.multiple_of((1 - bits[b]) * size, size) if halved else 0
        mine = pl.multiple_of(bits[b] * size, size) if halved else 0
        send = remote(
            held.at[:, pl.ds(other, size), :], landed[b], ws.at[b], wr.at[b], dp=partners[b]
        )
        send.start()
        send.wait_recv()
        sums[b][...] = (
            held[:, pl.ds(mine, size), :].astype(jnp.float32) + landed[b][...].astype(jnp.float32)
        ).astype(jnp.bfloat16)
        send.wait_send()
        held, offset = sums[b], offset + mine
    size = sizes[-1][0]
    here = pl.ds(pl.multiple_of(offset, size), size)
    own_w = pltpu.make_async_copy(held.at[me], w_all.at[me, here, :], own_sem.at[5])
    own_w.start()
    sent_w = []
    for k in range(1, n):
        copy = remote(
            held.at[peers[k - 1]], w_all.at[me, here, :], ps.at[k - 1], pr.at[k - 1], seq=peers[k - 1]
        )
        copy.start()
        sent_w.append(copy)

    for copy in sent_v:
        copy.start()

    def d_part(j):
        columns = jnp.concatenate(
            [g_all[h, :, j * HEAD : (j + 1) * HEAD] for h in range(HEADS)], axis=1
        )
        return lax.dot_general(
            columns, weights_s[:, j * HEADS * HEAD : (j + 1) * HEADS * HEAD], NT,
            preferred_element_type=jnp.float32,
        )

    own_g.wait()
    for copy in sent_g:
        copy.wait()
    d_s[...] = d_part(0) + d_part(1)
    inverse, unit, _ = normalized(
        pick(lambda b: chosen[me * n + b], lambda b: frames_s[b], frames_s.shape[2]), gain[...]
    )

    def d_input():
        for copy in sent_v:
            copy.wait()
        gained = (d_s[...] + d_part(2)) * gain[...]
        mean = jnp.mean(gained * unit, axis=-1, keepdims=True)
        d_out[...] = (inverse * (gained - unit * mean)).astype(jnp.bfloat16)

    own_w.wait()
    for copy in sent_w:
        copy.wait()
    spread = [b for b in reversed(range(count)) if sizes[b][1]]
    for b in spread:
        size = sizes[b][0]
        here = pl.ds(pl.multiple_of(offset, size), size)
        copy = remote(
            w_all.at[:, here, :], w_all.at[:, here, :], bs.at[b], br.at[b], dp=partners[b]
        )
        copy.start()
        if b == spread[-1]:
            d_input()
        copy.wait()
        offset = offset - bits[b] * size
    if not spread:
        d_input()

    for chunk in range(CHUNKS):
        across(0, 0, chunk, me).wait_send()
        for way in range(2):
            for hop in range(length - 1):
                @pl.when(can_send(way, hop))
                def _():
                    along(way, hop, chunk, me).wait_send()

                @pl.when(arrives(way, hop))
                def _():
                    across(way, hop + 1, chunk, me).wait_send()


def results_kernel(scale, d_in, w_in, d_out, w_out):
    d_out[0] = d_in[...]
    for h in range(HEADS):
        w_out[:, h * HEAD : (h + 1) * HEAD] = w_in[h].astype(jnp.float32) * scale


def results(scale, d_frames, w_all):
    rows, width = d_frames.shape
    n, w_rows, _ = w_all.shape
    return pl.pallas_call(
        functools.partial(results_kernel, scale),
        grid=(3,),
        in_specs=[
            pl.BlockSpec((rows, width), lambda j: (0, 0)),
            pl.BlockSpec((n, w_rows, HEAD), lambda j: (0, 0, j)),
        ],
        out_specs=(
            pl.BlockSpec((1, rows, width), lambda j: (0, 0, 0)),
            pl.BlockSpec((w_rows, HEADS * HEAD), lambda j: (0, j)),
        ),
        out_shape=(
            jax.ShapeDtypeStruct((1, rows, width), jnp.bfloat16),
            jax.ShapeDtypeStruct((w_rows, 3 * HEADS * HEAD), jnp.float32),
        ),
        name="results",
    )(d_frames, w_all)


def body(n, groups, layer_rows, doc_ids, packing, norm_gain, w_qkv, d_attn):
    width = w_qkv.shape[0]
    total = n * BLOCK
    rows = width // n
    sizes = halvings(rows, groups)
    count = len(sizes)
    dma = pltpu.SemaphoreType.DMA
    low = jnp.bfloat16
    hbm = pl.BlockSpec(memory_space=pl.ANY)
    vmem = pl.BlockSpec(memory_space=pltpu.VMEM)
    buffers = [pltpu.VMEM((n, size, 3 * HEAD), low) for size, _ in sizes]
    routes = dma((2, n // 2, CHUNKS))
    d_frames, w_all = pl.pallas_call(
        functools.partial(kernel, n, groups),
        out_shape=(
            jax.ShapeDtypeStruct((BLOCK, width), low),
            jax.ShapeDtypeStruct((n, rows, 3 * HEAD), low),
        ),
        in_specs=[vmem, hbm, vmem, hbm, hbm, hbm],
        out_specs=(vmem, hbm),
        scratch_shapes=[
            pltpu.VMEM((n, BLOCK, width), low),
            pltpu.VMEM((n, 1, BLOCK), jnp.int32),
            pltpu.VMEM((n, BLOCK, HEAD), low),
            pltpu.VMEM(w_qkv.shape, low),
            pltpu.VMEM((total, width), low),
            pltpu.VMEM((total, HEAD), low),
            pltpu.VMEM((total, HEAD), low),
            pltpu.VMEM((total, HEAD), low),
            pltpu.VMEM((total, HEAD), jnp.float32),
            pltpu.VMEM((total, HEAD), jnp.float32),
            pltpu.VMEM((total, 3 * HEAD), low),
            pltpu.VMEM((n, BLOCK, 3 * HEAD), low),
            pltpu.VMEM((n, BLOCK, 3 * HEAD), low),
            pltpu.VMEM((n, rows, 3 * HEAD), low),
            pltpu.VMEM((n * n, 1, HEAD), jnp.float32),
            pltpu.VMEM((BLOCK, width), jnp.float32),
            dma((6,)),
            *buffers, *buffers,
            routes, routes, routes, routes,
            dma((n,)), dma((n,)), dma((n,)), dma((n,)), dma((n,)), dma((n,)),
            dma((n,)), dma((n,)),
            dma((count,)), dma((count,)), dma((n,)), dma((n,)), dma((count,)), dma((count,)),
        ],
        compiler_params=pltpu.CompilerParams(
            collective_id=0, has_side_effects=True, vmem_limit_bytes=VMEM_LIMIT
        ),
        name="attention_backward",
    )(packing, layer_rows[0], norm_gain.reshape(1, -1), w_qkv, doc_ids, d_attn[0])
    return results(1.0 / math.sqrt(total * groups), d_frames, w_all)


def solution(mesh):
    return jax.shard_map(
        functools.partial(body, mesh.shape["seq"], mesh.shape["dp"]),
        mesh=mesh,
        in_specs=(
            P("dp", "seq", None),
            P("dp", "seq"),
            P("dp", None),
            P(),
            P(),
            P("dp", "seq", None),
        ),
        out_specs=(P("dp", "seq", None), P("seq", None)),
        check_vma=False,
    )
```

```python
import functools
import math

import jax
import jax.numpy as jnp
from jax import lax
from jax.experimental import pallas as pl
from jax.experimental.pallas import tpu as pltpu
from jax.sharding import PartitionSpec as P

HEADS = 8
HEAD = 128
BLOCK = 128
DOCS = 6
EPS = 1e-05
FACTOR = 1.0 / math.sqrt(HEAD)
MESH = pl.DeviceIdType.MESH
VMEM_LIMIT = 56 * 1024 * 1024
CHUNKS = 4
NT = (((1,), (1,)), ((), ()))
TN = (((0,), (0,)), ((), ()))


def remote(src, dst, send, recv, **where):
    return pltpu.make_async_remote_copy(
        src_ref=src, dst_ref=dst, send_sem=send, recv_sem=recv, device_id=where, device_id_type=MESH
    )


def normalized(frames, gain):
    values = frames.astype(jnp.float32)
    inverse = lax.rsqrt(jnp.mean(values * values, axis=-1, keepdims=True) + EPS)
    unit = values * inverse
    return inverse, unit, (unit * gain).astype(jnp.bfloat16)


def halvings(rows, groups):
    sizes = []
    for _ in range(groups.bit_length() - 1):
        halved = rows % 32 == 0
        rows = rows // 2 if halved else rows
        sizes.append((rows, halved))
    return sizes


def kernel(
    n, groups, packing, frames, gain, w_qkv, docs, grads, d_out, w_all,
    frames_s, docs_s, grads_s, weights_s, normed_s, q_s, k_s, v_s, prob_s, dscore_s,
    packed_s, g_s, g_send, g_all, w_part, chosen, d_s, own_sem, *scratch,
):
    sizes = halvings(w_part.shape[2], groups)
    count = len(sizes)
    landed, sums = scratch[:count], scratch[count : 2 * count]
    zs, zr, ys, yr, ds, dr, ts, tr, gs, gr, ws, wr, ps, pr, bs, br = scratch[2 * count :]
    me = lax.axis_index("seq")
    dp = lax.axis_index("dp")
    side = lax.rem(me, 2)
    place = me // 2
    partner = me + 1 - 2 * side
    length = n // 2
    part = BLOCK // CHUNKS
    head = lax.rem(me, HEADS)
    peers = [lax.rem(me + k, n) for k in range(1, n)]
    bits = [lax.rem(dp // (1 << b), 2) for b in range(count)]
    partners = [dp + (1 << b) * (1 - 2 * bits[b]) for b in range(count)]

    def head_of(device):
        start = pl.multiple_of(lax.rem(device, HEADS) * HEAD, HEAD)
        return grads.at[:, pl.ds(start, HEAD)]

    barrier = pltpu.get_barrier_semaphore()
    for peer in peers:
        pl.semaphore_signal(barrier, inc=1, device_id={"seq": peer}, device_id_type=MESH)
    for other in partners:
        pl.semaphore_signal(barrier, inc=1, device_id={"dp": other}, device_id_type=MESH)
    own_frames = pltpu.make_async_copy(frames, frames_s.at[me], own_sem.at[0])
    own_weights = pltpu.make_async_copy(w_qkv, weights_s, own_sem.at[1])
    own_grads = pltpu.make_async_copy(head_of(me), grads_s.at[me], own_sem.at[2])
    own_docs = pltpu.make_async_copy(docs, docs_s.at[me], own_sem.at[3])
    for copy in (own_frames, own_weights, own_grads, own_docs):
        copy.start()
    pl.semaphore_wait(barrier, n - 1 + count)

    def piece(block, chunk):
        return frames_s.at[block, pl.ds(chunk * part, part), :]

    def along(way, hop, chunk, block, source=None):
        return remote(
            piece(block, chunk) if source is None else source, piece(block, chunk),
            zs.at[way, hop, chunk], zr.at[way, hop, chunk], seq=me + (2 if way == 0 else -2),
        )

    def across(way, hop, chunk, block, source=None):
        return remote(
            piece(block, chunk) if source is None else source, piece(block, chunk),
            ys.at[way, hop, chunk], yr.at[way, hop, chunk], seq=partner,
        )

    def can_send(way, hop):
        if way == 0:
            return (place + 1 < length) & (place - hop >= 0)
        return (place - 1 >= 0) & (place + hop < length)

    def arrives(way, hop):
        return place - 1 - hop >= 0 if way == 0 else place + 1 + hop < length

    def origin(way, hop):
        return me - 2 * (hop + 1) if way == 0 else me + 2 * (hop + 1)

    for chunk in range(CHUNKS):
        source = frames.at[pl.ds(chunk * part, part), :]
        for way in range(2):
            @pl.when(can_send(way, 0))
            def _():
                along(way, 0, chunk, me, source).start()
        across(0, 0, chunk, me, source).start()
    small = []
    for k in range(1, n):
        small.append(remote(docs, docs_s.at[me], ds.at[k - 1], dr.at[k - 1], seq=peers[k - 1]))
        small.append(
            remote(head_of(peers[k - 1]), grads_s.at[me], ts.at[k - 1], tr.at[k - 1], seq=peers[k - 1])
        )
    for copy in small[::2]:
        copy.start()

    def project(block):
        rows = pl.ds(pl.multiple_of(block * BLOCK, BLOCK), BLOCK)
        normed = normalized(frames_s[block], gain[...])[2]
        normed_s[:, rows] = normed.T
        for j, kept in enumerate((q_s, k_s, v_s)):
            columns = pl.ds(pl.multiple_of((j * HEADS + head) * HEAD, HEAD), HEAD)
            kept[rows, :] = jnp.dot(
                normed, weights_s[:, columns], preferred_element_type=jnp.float32
            ).astype(jnp.bfloat16)

    order = packing[...]
    for r in range(n):
        for b in range(n):
            chosen[r * n + b] = jnp.broadcast_to(
                jnp.where(order[:, r : r + 1] == b, 1.0, 0.0), (1, HEAD)
            )
    own_frames.wait()
    own_weights.wait()
    project(me)
    for hop in range(length - 1):
        for chunk in range(CHUNKS):
            for way in range(2):
                @pl.when(arrives(way, hop))
                def _():
                    block = origin(way, hop)
                    along(way, hop, chunk, block).wait_recv()
                    if hop + 1 < length - 1:
                        @pl.when(can_send(way, hop + 1))
                        def _():
                            along(way, hop + 1, chunk, block).start()
                    across(way, hop + 1, chunk, block).start()
        for way in range(2):
            @pl.when(arrives(way, hop))
            def _():
                project(origin(way, hop))
        if hop == 0:
            for chunk in range(CHUNKS):
                across(0, 0, chunk, partner).wait_recv()
            project(partner)
    for copy in small[1::2]:
        copy.start()
    for hop in range(1, length):
        for way in range(2):
            @pl.when(arrives(way, hop - 1))
            def _():
                block = origin(way, hop - 1) + partner - me
                for chunk in range(CHUNKS):
                    across(way, hop, chunk, block).wait_recv()
                project(block)
    own_grads.wait()
    own_docs.wait()
    for copy in small:
        copy.wait()

    numbers = docs_s[...]
    counts = [
        jnp.sum(
            jnp.sum(jnp.where(numbers == d, 1.0, 0.0), axis=0), axis=-1, keepdims=True
        )
        for d in range(DOCS - 1)
    ]

    def first_of(block):
        own = docs_s[block]
        start = jnp.zeros(own.shape, jnp.float32)
        for d in range(DOCS - 1):
            start = start + jnp.where(own > d, counts[d], 0.0)
        return start.astype(jnp.int32)

    def pick(weight_of, block_of, width):
        total = None
        for b in range(n):
            weight = jnp.concatenate([weight_of(b).astype(jnp.bfloat16)] * (width // HEAD), axis=1)
            term = weight * block_of(b)
            total = term if total is None else total + term
        return total

    def grads_of(block):
        return pick(lambda r: chosen[r * n + block], lambda r: grads_s[r], HEAD)

    for i in range(n // 2):
        low, high = 2 * i * BLOCK, 2 * (i + 1) * BLOCK
        first = jnp.concatenate([first_of(2 * i), first_of(2 * i + 1)], axis=1)
        last = low + lax.broadcasted_iota(jnp.int32, (1, 2 * BLOCK), 1)
        pos = lax.broadcasted_iota(jnp.int32, (high, 2 * BLOCK), 0)
        q = q_s[low:high, :]
        g = jnp.concatenate([grads_of(2 * i), grads_of(2 * i + 1)], axis=0)
        packed_s[low:high, :] = g
        keys = k_s[:high, :]
        scores = lax.dot_general(keys, q, NT, preferred_element_type=jnp.float32)
        expon = jnp.where(
            (pos >= first) & (pos <= last),
            jnp.exp2(scores * (FACTOR * math.log2(math.e))),
            0.0,
        )
        prob = expon * (1.0 / jnp.sum(expon, axis=0, keepdims=True))
        prob_low = prob.astype(jnp.bfloat16)
        grad_prob = lax.dot_general(v_s[:high, :], g, NT, preferred_element_type=jnp.float32)
        delta = jnp.sum(prob_low.astype(jnp.float32) * grad_prob, axis=0, keepdims=True)
        dscore = (prob * (grad_prob - delta)).astype(jnp.bfloat16)
        prob_s[:high, low:high] = prob_low
        dscore_s[:high, low:high] = dscore
        dq = lax.dot_general(dscore, keys, TN, preferred_element_type=jnp.float32)
        g_s[0, low:high, :] = (dq * FACTOR).astype(jnp.bfloat16)

    def key_sums(p, kept, other_of, factor):
        for j in range(n // 2):
            low, high = 2 * j * BLOCK, 2 * (j + 1) * BLOCK
            total = jnp.dot(
                kept[low:high, low:], other_of(low), preferred_element_type=jnp.float32
            )
            g_s[p, low:high, :] = (total * factor).astype(jnp.bfloat16)

    def stage(p):
        for r in range(n):
            g_send[p, r] = pick(
                lambda b: chosen[r * n + b], lambda b: g_s[p, b * BLOCK : (b + 1) * BLOCK, :], HEAD
            )

    def halve(p, b, held):
        size, halved = sizes[b]
        other = pl.multiple_of((1 - bits[b]) * size, size) if halved else 0
        send = remote(
            held.at[p, :, pl.ds(other, size), :], landed[b].at[p], ws.at[b, p], wr.at[b, p],
            dp=partners[b],
        )
        send.start()
        return send

    def weight_part(p):
        w_part[p] = (
            jnp.dot(normed_s[...], g_s[p], preferred_element_type=jnp.float32)
            .astype(jnp.bfloat16)
            .reshape(w_part.shape[1:])
        )
        return halve(p, 0, w_part)

    def grad_copies(p):
        own_g[p].start()
        return [
            remote(
                g_send.at[p, peer], g_all.at[p, me], gs.at[p, k], gr.at[p, k], seq=peer
            )
            for k, peer in enumerate(peers)
        ]

    own_g = [
        pltpu.make_async_copy(g_send.at[p, me], g_all.at[p, me], own_sem.at[4 + p]) for p in range(3)
    ]
    sent_g, halves = [], []
    for p in range(3):
        if p == 1:
            key_sums(1, dscore_s, lambda low: q_s[low:, :], FACTOR)
        if p == 2:
            key_sums(2, prob_s, lambda low: packed_s[low:, :], 1.0)
        stage(p)
        sent_g.append(grad_copies(p))
        if p < 2:
            for copy in sent_g[p]:
                copy.start()
        halves.append(weight_part(p))

    held, offset = w_part, 0
    for b, (size, halved) in enumerate(sizes):
        mine = pl.multiple_of(bits[b] * size, size) if halved else 0
        later = []
        for p in range(3):
            halves[p].wait_recv()
            sums[b][p] = (
                held[p, :, pl.ds(mine, size), :].astype(jnp.float32)
                + landed[b][p].astype(jnp.float32)
            ).astype(jnp.bfloat16)
            if b + 1 < count:
                later.append(halve(p, b + 1, sums[b]))
            halves[p].wait_send()
        halves, held, offset = later, sums[b], offset + mine
    size = sizes[-1][0]
    here = pl.ds(pl.multiple_of(offset, size), size)
    sent_w, own_w = [], []
    for p in range(3):
        own = pltpu.make_async_copy(held.at[p, me], w_all.at[p, me, here, :], own_sem.at[7 + p])
        own.start()
        own_w.append(own)
        sent_w.append([
            remote(
                held.at[p, peer], w_all.at[p, me, here, :], ps.at[p, k], pr.at[p, k], seq=peer
            )
            for k, peer in enumerate(peers)
        ])
        for copy in sent_w[p]:
            copy.start()
    for copy in sent_g[2]:
        copy.start()

    def d_part(j):
        columns = jnp.concatenate(
            [g_all[j, h] for h in range(HEADS)], axis=1
        )
        return lax.dot_general(
            columns, weights_s[:, j * HEADS * HEAD : (j + 1) * HEADS * HEAD], NT,
            preferred_element_type=jnp.float32,
        )

    for p in range(2):
        for copy in [own_g[p]] + sent_g[p]:
            copy.wait()
    d_s[...] = d_part(0) + d_part(1)
    inverse, unit, _ = normalized(
        pick(lambda b: chosen[me * n + b], lambda b: frames_s[b], frames_s.shape[2]), gain[...]
    )

    def d_input():
        for copy in [own_g[2]] + sent_g[2]:
            copy.wait()
        gained = (d_s[...] + d_part(2)) * gain[...]
        mean = jnp.mean(gained * unit, axis=-1, keepdims=True)
        d_out[...] = (inverse * (gained - unit * mean)).astype(jnp.bfloat16)

    spread = [b for b in reversed(range(count)) if sizes[b][1]]

    def widen(p, b, offset):
        size = sizes[b][0]
        here = pl.ds(pl.multiple_of(offset, size), size)
        copy = remote(
            w_all.at[p, :, here, :], w_all.at[p, :, here, :], bs.at[b, p], br.at[b, p],
            dp=partners[b],
        )
        copy.start()
        return copy

    spreading = []
    for p in range(3):
        for copy in [own_w[p]] + sent_w[p]:
            copy.wait()
        if spread:
            spreading.append(widen(p, spread[0], offset))
    for place_of, b in enumerate(spread):
        offset = offset - bits[b] * sizes[b][0]
        later = []
        for p in range(3):
            spreading[p].wait()
            if place_of + 1 < len(spread):
                later.append(widen(p, spread[place_of + 1], offset))
        spreading = later
        if place_of + 2 == len(spread):
            d_input()
    if len(spread) < 2:
        d_input()

    for chunk in range(CHUNKS):
        across(0, 0, chunk, me).wait_send()
        for way in range(2):
            for hop in range(length - 1):
                @pl.when(can_send(way, hop))
                def _():
                    along(way, hop, chunk, me).wait_send()

                @pl.when(arrives(way, hop))
                def _():
                    across(way, hop + 1, chunk, me).wait_send()


def results_kernel(scale, d_in, w_in, d_out, w_out):
    d_out[0] = d_in[...]
    for h in range(HEADS):
        w_out[:, h * HEAD : (h + 1) * HEAD] = w_in[0, h].astype(jnp.float32) * scale


def results(scale, d_frames, w_all):
    rows, width = d_frames.shape
    _, n, w_rows, _ = w_all.shape
    return pl.pallas_call(
        functools.partial(results_kernel, scale),
        grid=(3,),
        in_specs=[
            pl.BlockSpec((rows, width), lambda j: (0, 0)),
            pl.BlockSpec((1, n, w_rows, HEAD), lambda j: (j, 0, 0, 0)),
        ],
        out_specs=(
            pl.BlockSpec((1, rows, width), lambda j: (0, 0, 0)),
            pl.BlockSpec((w_rows, HEADS * HEAD), lambda j: (0, j)),
        ),
        out_shape=(
            jax.ShapeDtypeStruct((1, rows, width), jnp.bfloat16),
            jax.ShapeDtypeStruct((w_rows, 3 * HEADS * HEAD), jnp.float32),
        ),
        name="results",
    )(d_frames, w_all)


def body(n, groups, layer_rows, doc_ids, packing, norm_gain, w_qkv, d_attn):
    width = w_qkv.shape[0]
    total = n * BLOCK
    rows = width // n
    sizes = halvings(rows, groups)
    count = len(sizes)
    dma = pltpu.SemaphoreType.DMA
    low = jnp.bfloat16
    hbm = pl.BlockSpec(memory_space=pl.ANY)
    vmem = pl.BlockSpec(memory_space=pltpu.VMEM)
    buffers = [pltpu.VMEM((3, n, size, HEAD), low) for size, _ in sizes]
    routes = dma((2, n // 2, CHUNKS))
    d_frames, w_all = pl.pallas_call(
        functools.partial(kernel, n, groups),
        out_shape=(
            jax.ShapeDtypeStruct((BLOCK, width), low),
            jax.ShapeDtypeStruct((3, n, rows, HEAD), low),
        ),
        in_specs=[vmem, hbm, vmem, hbm, hbm, hbm],
        out_specs=(vmem, hbm),
        scratch_shapes=[
            pltpu.VMEM((n, BLOCK, width), low),
            pltpu.VMEM((n, 1, BLOCK), jnp.int32),
            pltpu.VMEM((n, BLOCK, HEAD), low),
            pltpu.VMEM(w_qkv.shape, low),
            pltpu.VMEM((width, total), low),
            pltpu.VMEM((total, HEAD), low),
            pltpu.VMEM((total, HEAD), low),
            pltpu.VMEM((total, HEAD), low),
            pltpu.VMEM((total, total), low),
            pltpu.VMEM((total, total), low),
            pltpu.VMEM((total, HEAD), low),
            pltpu.VMEM((3, total, HEAD), low),
            pltpu.VMEM((3, n, BLOCK, HEAD), low),
            pltpu.VMEM((3, n, BLOCK, HEAD), low),
            pltpu.VMEM((3, n, rows, HEAD), low),
            pltpu.VMEM((n * n, 1, HEAD), jnp.float32),
            pltpu.VMEM((BLOCK, width), jnp.float32),
            dma((10,)),
            *buffers, *buffers,
            routes, routes, routes, routes,
            dma((n,)), dma((n,)), dma((n,)), dma((n,)), dma((3, n)), dma((3, n)),
            dma((count, 3)), dma((count, 3)), dma((3, n)), dma((3, n)), dma((count, 3)), dma((count, 3)),
        ],
        compiler_params=pltpu.CompilerParams(
            collective_id=0, has_side_effects=True, vmem_limit_bytes=VMEM_LIMIT
        ),
        name="attention_backward",
    )(packing, layer_rows[0], norm_gain.reshape(1, -1), w_qkv, doc_ids, d_attn[0])
    return results(1.0 / math.sqrt(total * groups), d_frames, w_all)


def solution(mesh):
    return jax.shard_map(
        functools.partial(body, mesh.shape["seq"], mesh.shape["dp"]),
        mesh=mesh,
        in_specs=(
            P("dp", "seq", None),
            P("dp", "seq"),
            P("dp", None),
            P(),
            P(),
            P("dp", "seq", None),
        ),
        out_specs=(P("dp", "seq", None), P("seq", None)),
        check_vma=False,
    )
```

```python
import functools
import math

import jax
import jax.numpy as jnp
from jax import lax
from jax.experimental import pallas as pl
from jax.experimental.pallas import tpu as pltpu
from jax.sharding import PartitionSpec as P

HEADS = 8
HEAD = 128
BLOCK = 128
DOCS = 6
EPS = 1e-05
FACTOR = 1.0 / math.sqrt(HEAD)
MESH = pl.DeviceIdType.MESH
VMEM_LIMIT = 56 * 1024 * 1024
CHUNKS = 4
TWINS = CHUNKS // 2
NT = (((1,), (1,)), ((), ()))
TN = (((0,), (0,)), ((), ()))


def remote(src, dst, send, recv, **where):
    return pltpu.make_async_remote_copy(
        src_ref=src, dst_ref=dst, send_sem=send, recv_sem=recv, device_id=where, device_id_type=MESH
    )


def normalized(frames, gain):
    values = frames.astype(jnp.float32)
    inverse = lax.rsqrt(jnp.mean(values * values, axis=-1, keepdims=True) + EPS)
    unit = values * inverse
    return inverse, unit, (unit * gain).astype(jnp.bfloat16)


def halvings(rows, groups):
    sizes = []
    for _ in range(groups.bit_length() - 1):
        halved = rows % 32 == 0
        rows = rows // 2 if halved else rows
        sizes.append((rows, halved))
    return sizes


def kernel(
    n, groups, packing, frames, gain, w_qkv, docs, grads, d_out, w_all,
    frames_s, docs_s, grads_s, weights_s, normed_s, q_s, k_s, v_s, prob_s, dscore_s,
    packed_s, g_s, g_send, g_all, w_part, chosen, d_s, own_sem, *scratch,
):
    sizes = halvings(w_part.shape[2], groups)
    count = len(sizes)
    landed, sums = scratch[:count], scratch[count : 2 * count]
    zs, zr, ys, yr, ds, dr, ts, tr, gs, gr, ws, wr, ps, pr, bs, br = scratch[2 * count :]
    me = lax.axis_index("seq")
    dp = lax.axis_index("dp")
    side = lax.rem(me, 2)
    place = me // 2
    partner = me + 1 - 2 * side
    length = n // 2
    part = BLOCK // CHUNKS
    head = lax.rem(me, HEADS)
    peers = [lax.rem(me + k, n) for k in range(1, n)]
    bits = [lax.rem(dp // (1 << b), 2) for b in range(count)]
    partners = [dp + (1 << b) * (1 - 2 * bits[b]) for b in range(count)]

    def head_of(device):
        start = pl.multiple_of(lax.rem(device, HEADS) * HEAD, HEAD)
        return grads.at[:, pl.ds(start, HEAD)]

    barrier = pltpu.get_barrier_semaphore()
    for peer in peers:
        pl.semaphore_signal(barrier, inc=1, device_id={"seq": peer}, device_id_type=MESH)
    for other in partners:
        pl.semaphore_signal(barrier, inc=1, device_id={"dp": other}, device_id_type=MESH)
    own_frames = pltpu.make_async_copy(frames, frames_s.at[me], own_sem.at[0])
    own_weights = pltpu.make_async_copy(w_qkv, weights_s, own_sem.at[1])
    own_grads = pltpu.make_async_copy(head_of(me), grads_s.at[me], own_sem.at[2])
    own_docs = pltpu.make_async_copy(docs, docs_s.at[me], own_sem.at[3])
    for copy in (own_frames, own_weights, own_grads, own_docs):
        copy.start()
    pl.semaphore_wait(barrier, n - 1 + count)

    def piece(block, chunk):
        return frames_s.at[block, pl.ds(chunk * part, part), :]

    def along(way, hop, chunk, block, source=None):
        return remote(
            piece(block, chunk) if source is None else source, piece(block, chunk),
            zs.at[way, hop, chunk], zr.at[way, hop, chunk], seq=me + (2 if way == 0 else -2),
        )

    def across(way, hop, chunk, block, source=None):
        return remote(
            piece(block, chunk) if source is None else source, piece(block, chunk),
            ys.at[way, hop, chunk], yr.at[way, hop, chunk], seq=partner,
        )

    def twin(way, chunk):
        return remote(
            piece(partner, chunk), piece(partner, chunk),
            ys.at[way, 1, chunk], yr.at[way, 1, chunk], seq=me + (2 if way == 0 else -2),
        )

    def can_send(way, hop):
        if way == 0:
            return (place + 1 < length) & (place - hop >= 0)
        return (place - 1 >= 0) & (place + hop < length)

    def arrives(way, hop):
        return place - 1 - hop >= 0 if way == 0 else place + 1 + hop < length

    def origin(way, hop):
        return me - 2 * (hop + 1) if way == 0 else me + 2 * (hop + 1)

    for chunk in range(CHUNKS):
        source = frames.at[pl.ds(chunk * part, part), :]
        for way in range(2):
            @pl.when(can_send(way, 0))
            def _():
                along(way, 0, chunk, me, source).start()
    for chunk in reversed(range(CHUNKS)):
        across(0, 0, chunk, me, frames.at[pl.ds(chunk * part, part), :]).start()
    small = []
    for k in range(1, n):
        small.append(remote(docs, docs_s.at[me], ds.at[k - 1], dr.at[k - 1], seq=peers[k - 1]))
        small.append(
            remote(head_of(peers[k - 1]), grads_s.at[me], ts.at[k - 1], tr.at[k - 1], seq=peers[k - 1])
        )
    for copy in small[::2]:
        copy.start()

    def project(block):
        rows = pl.ds(pl.multiple_of(block * BLOCK, BLOCK), BLOCK)
        normed = normalized(frames_s[block], gain[...])[2]
        normed_s[:, rows] = normed.T
        for j, kept in enumerate((q_s, k_s, v_s)):
            columns = pl.ds(pl.multiple_of((j * HEADS + head) * HEAD, HEAD), HEAD)
            kept[rows, :] = jnp.dot(
                normed, weights_s[:, columns], preferred_element_type=jnp.float32
            ).astype(jnp.bfloat16)

    order = packing[...]
    for r in range(n):
        for b in range(n):
            chosen[r * n + b] = jnp.broadcast_to(
                jnp.where(order[:, r : r + 1] == b, 1.0, 0.0), (1, HEAD)
            )
    own_frames.wait()
    own_weights.wait()
    project(me)
    for hop in range(length - 1):
        for chunk in range(CHUNKS):
            for way in range(2):
                @pl.when(arrives(way, hop))
                def _():
                    block = origin(way, hop)
                    along(way, hop, chunk, block).wait_recv()
                    if hop + 1 < length - 1:
                        @pl.when(can_send(way, hop + 1))
                        def _():
                            along(way, hop + 1, chunk, block).start()
                    if hop > 0 or chunk < TWINS:
                        across(way, hop + 1, chunk, block).start()
        if hop == 0:
            for chunk in reversed(range(TWINS, CHUNKS)):
                across(0, 0, chunk, partner).wait_recv()
                for way in range(2):
                    @pl.when(can_send(way, 0))
                    def _():
                        twin(way, chunk).start()
        for way in range(2):
            @pl.when(arrives(way, hop))
            def _():
                project(origin(way, hop))
        if hop == 0:
            for chunk in range(TWINS):
                across(0, 0, chunk, partner).wait_recv()
            project(partner)
    for copy in small[1::2]:
        copy.start()
    for hop in range(1, length):
        for way in range(2):
            @pl.when(arrives(way, hop - 1))
            def _():
                block = origin(way, hop - 1) + partner - me
                for chunk in range(CHUNKS):
                    across(way, hop, chunk, block).wait_recv()
                project(block)
    own_grads.wait()
    own_docs.wait()
    for copy in small:
        copy.wait()

    numbers = docs_s[...]
    counts = [
        jnp.sum(
            jnp.sum(jnp.where(numbers == d, 1.0, 0.0), axis=0), axis=-1, keepdims=True
        )
        for d in range(DOCS - 1)
    ]

    def first_of(block):
        own = docs_s[block]
        start = jnp.zeros(own.shape, jnp.float32)
        for d in range(DOCS - 1):
            start = start + jnp.where(own > d, counts[d], 0.0)
        return start.astype(jnp.int32)

    def pick(weight_of, block_of, width):
        total = None
        for b in range(n):
            weight = jnp.concatenate([weight_of(b).astype(jnp.bfloat16)] * (width // HEAD), axis=1)
            term = weight * block_of(b)
            total = term if total is None else total + term
        return total

    def grads_of(block):
        return pick(lambda r: chosen[r * n + block], lambda r: grads_s[r], HEAD)

    for i in range(n // 2):
        low, high = 2 * i * BLOCK, 2 * (i + 1) * BLOCK
        first = jnp.concatenate([first_of(2 * i), first_of(2 * i + 1)], axis=1)
        last = low + lax.broadcasted_iota(jnp.int32, (1, 2 * BLOCK), 1)
        pos = lax.broadcasted_iota(jnp.int32, (high, 2 * BLOCK), 0)
        q = q_s[low:high, :]
        g = jnp.concatenate([grads_of(2 * i), grads_of(2 * i + 1)], axis=0)
        packed_s[low:high, :] = g
        keys = k_s[:high, :]
        scores = lax.dot_general(keys, q, NT, preferred_element_type=jnp.float32)
        expon = jnp.where(
            (pos >= first) & (pos <= last),
            jnp.exp2(scores * (FACTOR * math.log2(math.e))),
            0.0,
        )
        prob = expon * (1.0 / jnp.sum(expon, axis=0, keepdims=True))
        prob_low = prob.astype(jnp.bfloat16)
        grad_prob = lax.dot_general(v_s[:high, :], g, NT, preferred_element_type=jnp.float32)
        delta = jnp.sum(prob_low.astype(jnp.float32) * grad_prob, axis=0, keepdims=True)
        dscore = (prob * (grad_prob - delta)).astype(jnp.bfloat16)
        prob_s[:high, low:high] = prob_low
        dscore_s[:high, low:high] = dscore
        dq = lax.dot_general(dscore, keys, TN, preferred_element_type=jnp.float32)
        g_s[0, low:high, :] = (dq * FACTOR).astype(jnp.bfloat16)

    def key_sums(p, kept, other_of, factor):
        for j in range(n // 2):
            low, high = 2 * j * BLOCK, 2 * (j + 1) * BLOCK
            total = jnp.dot(
                kept[low:high, low:], other_of(low), preferred_element_type=jnp.float32
            )
            g_s[p, low:high, :] = (total * factor).astype(jnp.bfloat16)

    def stage(p):
        for r in range(n):
            g_send[p, r] = pick(
                lambda b: chosen[r * n + b], lambda b: g_s[p, b * BLOCK : (b + 1) * BLOCK, :], HEAD
            )

    def halve(p, b, held):
        size, halved = sizes[b]
        other = pl.multiple_of((1 - bits[b]) * size, size) if halved else 0
        send = remote(
            held.at[p, :, pl.ds(other, size), :], landed[b].at[p], ws.at[b, p], wr.at[b, p],
            dp=partners[b],
        )
        send.start()
        return send

    def weight_part(p):
        w_part[p] = (
            jnp.dot(normed_s[...], g_s[p], preferred_element_type=jnp.float32)
            .astype(jnp.bfloat16)
            .reshape(w_part.shape[1:])
        )
        return halve(p, 0, w_part)

    def grad_copies(p):
        own_g[p].start()
        return [
            remote(
                g_send.at[p, peer], g_all.at[p, me], gs.at[p, k], gr.at[p, k], seq=peer
            )
            for k, peer in enumerate(peers)
        ]

    own_g = [
        pltpu.make_async_copy(g_send.at[p, me], g_all.at[p, me], own_sem.at[4 + p]) for p in range(3)
    ]
    sent_g, halves = [], []
    for p in range(3):
        if p == 1:
            key_sums(1, dscore_s, lambda low: q_s[low:, :], FACTOR)
        if p == 2:
            key_sums(2, prob_s, lambda low: packed_s[low:, :], 1.0)
        stage(p)
        sent_g.append(grad_copies(p))
        if p < 2:
            for copy in sent_g[p]:
                copy.start()
        halves.append(weight_part(p))

    held, offset = w_part, 0
    for b, (size, halved) in enumerate(sizes):
        mine = pl.multiple_of(bits[b] * size, size) if halved else 0
        later = []
        for p in range(3):
            halves[p].wait_recv()
            sums[b][p] = (
                held[p, :, pl.ds(mine, size), :].astype(jnp.float32)
                + landed[b][p].astype(jnp.float32)
            ).astype(jnp.bfloat16)
            if b + 1 < count:
                later.append(halve(p, b + 1, sums[b]))
            halves[p].wait_send()
        halves, held, offset = later, sums[b], offset + mine
    size = sizes[-1][0]
    here = pl.ds(pl.multiple_of(offset, size), size)
    sent_w, own_w = [], []
    for p in range(3):
        own = pltpu.make_async_copy(held.at[p, me], w_all.at[p, me, here, :], own_sem.at[7 + p])
        own.start()
        own_w.append(own)
        sent_w.append([
            remote(
                held.at[p, peer], w_all.at[p, me, here, :], ps.at[p, k], pr.at[p, k], seq=peer
            )
            for k, peer in enumerate(peers)
        ])
        for copy in sent_w[p]:
            copy.start()
    for copy in sent_g[2]:
        copy.start()

    def d_part(j):
        columns = jnp.concatenate(
            [g_all[j, h] for h in range(HEADS)], axis=1
        )
        return lax.dot_general(
            columns, weights_s[:, j * HEADS * HEAD : (j + 1) * HEADS * HEAD], NT,
            preferred_element_type=jnp.float32,
        )

    for p in range(2):
        for copy in [own_g[p]] + sent_g[p]:
            copy.wait()
    d_s[...] = d_part(0) + d_part(1)
    inverse, unit, _ = normalized(
        pick(lambda b: chosen[me * n + b], lambda b: frames_s[b], frames_s.shape[2]), gain[...]
    )

    def d_input():
        for copy in [own_g[2]] + sent_g[2]:
            copy.wait()
        gained = (d_s[...] + d_part(2)) * gain[...]
        mean = jnp.mean(gained * unit, axis=-1, keepdims=True)
        d_out[...] = (inverse * (gained - unit * mean)).astype(jnp.bfloat16)

    spread = [b for b in reversed(range(count)) if sizes[b][1]]

    def widen(p, b, offset):
        size = sizes[b][0]
        here = pl.ds(pl.multiple_of(offset, size), size)
        copy = remote(
            w_all.at[p, :, here, :], w_all.at[p, :, here, :], bs.at[b, p], br.at[b, p],
            dp=partners[b],
        )
        copy.start()
        return copy

    spreading = []
    for p in range(3):
        for copy in [own_w[p]] + sent_w[p]:
            copy.wait()
        if spread:
            spreading.append(widen(p, spread[0], offset))
    for place_of, b in enumerate(spread):
        offset = offset - bits[b] * sizes[b][0]
        later = []
        for p in range(3):
            spreading[p].wait()
            if place_of + 1 < len(spread):
                later.append(widen(p, spread[place_of + 1], offset))
        spreading = later
        if place_of + 2 == len(spread):
            d_input()
    if len(spread) < 2:
        d_input()

    for chunk in range(CHUNKS):
        across(0, 0, chunk, me).wait_send()
        for way in range(2):
            for hop in range(length - 1):
                @pl.when(can_send(way, hop))
                def _():
                    along(way, hop, chunk, me).wait_send()

                if hop == 0 and chunk >= TWINS:
                    @pl.when(can_send(way, 0))
                    def _():
                        twin(way, chunk).wait_send()
                else:
                    @pl.when(arrives(way, hop))
                    def _():
                        across(way, hop + 1, chunk, me).wait_send()


def results_kernel(scale, d_in, w_in, d_out, w_out):
    d_out[0] = d_in[...]
    for h in range(HEADS):
        w_out[:, h * HEAD : (h + 1) * HEAD] = w_in[0, h].astype(jnp.float32) * scale


def results(scale, d_frames, w_all):
    rows, width = d_frames.shape
    _, n, w_rows, _ = w_all.shape
    return pl.pallas_call(
        functools.partial(results_kernel, scale),
        grid=(3,),
        in_specs=[
            pl.BlockSpec((rows, width), lambda j: (0, 0)),
            pl.BlockSpec((1, n, w_rows, HEAD), lambda j: (j, 0, 0, 0)),
        ],
        out_specs=(
            pl.BlockSpec((1, rows, width), lambda j: (0, 0, 0)),
            pl.BlockSpec((w_rows, HEADS * HEAD), lambda j: (0, j)),
        ),
        out_shape=(
            jax.ShapeDtypeStruct((1, rows, width), jnp.bfloat16),
            jax.ShapeDtypeStruct((w_rows, 3 * HEADS * HEAD), jnp.float32),
        ),
        name="results",
    )(d_frames, w_all)


def body(n, groups, layer_rows, doc_ids, packing, norm_gain, w_qkv, d_attn):
    width = w_qkv.shape[0]
    total = n * BLOCK
    rows = width // n
    sizes = halvings(rows, groups)
    count = len(sizes)
    dma = pltpu.SemaphoreType.DMA
    low = jnp.bfloat16
    hbm = pl.BlockSpec(memory_space=pl.ANY)
    vmem = pl.BlockSpec(memory_space=pltpu.VMEM)
    buffers = [pltpu.VMEM((3, n, size, HEAD), low) for size, _ in sizes]
    routes = dma((2, n // 2, CHUNKS))
    d_frames, w_all = pl.pallas_call(
        functools.partial(kernel, n, groups),
        out_shape=(
            jax.ShapeDtypeStruct((BLOCK, width), low),
            jax.ShapeDtypeStruct((3, n, rows, HEAD), low),
        ),
        in_specs=[vmem, hbm, vmem, hbm, hbm, hbm],
        out_specs=(vmem, hbm),
        scratch_shapes=[
            pltpu.VMEM((n, BLOCK, width), low),
            pltpu.VMEM((n, 1, BLOCK), jnp.int32),
            pltpu.VMEM((n, BLOCK, HEAD), low),
            pltpu.VMEM(w_qkv.shape, low),
            pltpu.VMEM((width, total), low),
            pltpu.VMEM((total, HEAD), low),
            pltpu.VMEM((total, HEAD), low),
            pltpu.VMEM((total, HEAD), low),
            pltpu.VMEM((total, total), low),
            pltpu.VMEM((total, total), low),
            pltpu.VMEM((total, HEAD), low),
            pltpu.VMEM((3, total, HEAD), low),
            pltpu.VMEM((3, n, BLOCK, HEAD), low),
            pltpu.VMEM((3, n, BLOCK, HEAD), low),
            pltpu.VMEM((3, n, rows, HEAD), low),
            pltpu.VMEM((n * n, 1, HEAD), jnp.float32),
            pltpu.VMEM((BLOCK, width), jnp.float32),
            dma((10,)),
            *buffers, *buffers,
            routes, routes, routes, routes,
            dma((n,)), dma((n,)), dma((n,)), dma((n,)), dma((3, n)), dma((3, n)),
            dma((count, 3)), dma((count, 3)), dma((3, n)), dma((3, n)), dma((count, 3)), dma((count, 3)),
        ],
        compiler_params=pltpu.CompilerParams(
            collective_id=0, has_side_effects=True, vmem_limit_bytes=VMEM_LIMIT
        ),
        name="attention_backward",
    )(packing, layer_rows[0], norm_gain.reshape(1, -1), w_qkv, doc_ids, d_attn[0])
    return results(1.0 / math.sqrt(total * groups), d_frames, w_all)


def solution(mesh):
    return jax.shard_map(
        functools.partial(body, mesh.shape["seq"], mesh.shape["dp"]),
        mesh=mesh,
        in_specs=(
            P("dp", "seq", None),
            P("dp", "seq"),
            P("dp", None),
            P(),
            P(),
            P("dp", "seq", None),
        ),
        out_specs=(P("dp", "seq", None), P("seq", None)),
        check_vma=False,
    )
```

```python
import functools
import math

import jax
import jax.numpy as jnp
from jax import lax
from jax.experimental import pallas as pl
from jax.experimental.pallas import tpu as pltpu
from jax.sharding import PartitionSpec as P

HEADS = 8
HEAD = 128
BLOCK = 128
DOCS = 6
EPS = 1e-05
FACTOR = 1.0 / math.sqrt(HEAD)
MESH = pl.DeviceIdType.MESH
VMEM_LIMIT = 56 * 1024 * 1024
CHUNKS = 4
NT = (((1,), (1,)), ((), ()))
TN = (((0,), (0,)), ((), ()))


def remote(src, dst, send, recv, **where):
    return pltpu.make_async_remote_copy(
        src_ref=src, dst_ref=dst, send_sem=send, recv_sem=recv, device_id=where, device_id_type=MESH
    )


def normalized(frames, gain):
    values = frames.astype(jnp.float32)
    inverse = lax.rsqrt(jnp.mean(values * values, axis=-1, keepdims=True) + EPS)
    unit = values * inverse
    return inverse, unit, (unit * gain).astype(jnp.bfloat16)


def halvings(rows, groups):
    sizes = []
    for _ in range(groups.bit_length() - 1):
        halved = rows % 32 == 0
        rows = rows // 2 if halved else rows
        sizes.append((rows, halved))
    return sizes


def kernel(
    n, groups, packing, frames, gain, w_qkv, docs, grads, d_out, w_all,
    frames_s, docs_s, grads_s, weights_s, normed_s, q_s, k_s, v_s, prob_s, dscore_s,
    packed_s, g_s, g_send, g_all, w_part, chosen, d_s, own_sem, *scratch,
):
    sizes = halvings(w_part.shape[2], groups)
    count = len(sizes)
    landed, sums = scratch[:count], scratch[count : 2 * count]
    zs, zr, ys, yr, ds, dr, ts, tr, gs, gr, ws, wr, ps, pr, bs, br = scratch[2 * count :]
    me = lax.axis_index("seq")
    dp = lax.axis_index("dp")
    side = lax.rem(me, 2)
    place = me // 2
    partner = me + 1 - 2 * side
    length = n // 2
    part = BLOCK // CHUNKS
    head = lax.rem(me, HEADS)
    peers = [lax.rem(me + k, n) for k in range(1, n)]
    bits = [lax.rem(dp // (1 << b), 2) for b in range(count)]
    partners = [dp + (1 << b) * (1 - 2 * bits[b]) for b in range(count)]

    def head_of(device):
        start = pl.multiple_of(lax.rem(device, HEADS) * HEAD, HEAD)
        return grads.at[:, pl.ds(start, HEAD)]

    barrier = pltpu.get_barrier_semaphore()
    for peer in peers:
        pl.semaphore_signal(barrier, inc=1, device_id={"seq": peer}, device_id_type=MESH)
    for other in partners:
        pl.semaphore_signal(barrier, inc=1, device_id={"dp": other}, device_id_type=MESH)
    own_frames = pltpu.make_async_copy(frames, frames_s.at[me], own_sem.at[0])
    own_weights = pltpu.make_async_copy(w_qkv, weights_s, own_sem.at[1])
    own_grads = pltpu.make_async_copy(head_of(me), grads_s.at[me], own_sem.at[2])
    own_docs = pltpu.make_async_copy(docs, docs_s.at[me], own_sem.at[3])
    for copy in (own_frames, own_weights, own_grads, own_docs):
        copy.start()
    pl.semaphore_wait(barrier, n - 1 + count)

    def piece(block, chunk):
        return frames_s.at[block, pl.ds(chunk * part, part), :]

    def along(way, hop, chunk, block, source=None):
        return remote(
            piece(block, chunk) if source is None else source, piece(block, chunk),
            zs.at[way, hop, chunk], zr.at[way, hop, chunk], seq=me + (2 if way == 0 else -2),
        )

    def across(way, hop, chunk, block, source=None):
        return remote(
            piece(block, chunk) if source is None else source, piece(block, chunk),
            ys.at[way, hop, chunk], yr.at[way, hop, chunk], seq=partner,
        )

    def can_send(way, hop):
        if way == 0:
            return (place + 1 < length) & (place - hop >= 0)
        return (place - 1 >= 0) & (place + hop < length)

    def arrives(way, hop):
        return place - 1 - hop >= 0 if way == 0 else place + 1 + hop < length

    def origin(way, hop):
        return me - 2 * (hop + 1) if way == 0 else me + 2 * (hop + 1)

    for chunk in range(CHUNKS):
        source = frames.at[pl.ds(chunk * part, part), :]
        for way in range(2):
            @pl.when(can_send(way, 0))
            def _():
                along(way, 0, chunk, me, source).start()
        across(0, 0, chunk, me, source).start()
    small = []
    for k in range(1, n):
        small.append(remote(docs, docs_s.at[me], ds.at[k - 1], dr.at[k - 1], seq=peers[k - 1]))
        small.append(
            remote(head_of(peers[k - 1]), grads_s.at[me], ts.at[k - 1], tr.at[k - 1], seq=peers[k - 1])
        )
    for copy in small[::2]:
        copy.start()

    def project(block):
        rows = pl.ds(pl.multiple_of(block * BLOCK, BLOCK), BLOCK)
        normed = normalized(frames_s[block], gain[...])[2]
        normed_s[:, rows] = normed.T
        for j, kept in enumerate((q_s, k_s, v_s)):
            columns = pl.ds(pl.multiple_of((j * HEADS + head) * HEAD, HEAD), HEAD)
            kept[rows, :] = jnp.dot(
                normed, weights_s[:, columns], preferred_element_type=jnp.float32
            ).astype(jnp.bfloat16)

    order = packing[...]
    for r in range(n):
        for b in range(n):
            chosen[r * n + b] = jnp.broadcast_to(
                jnp.where(order[:, r : r + 1] == b, 1.0, 0.0), (1, HEAD)
            )
    own_frames.wait()
    own_weights.wait()
    project(me)
    for hop in range(length - 1):
        for chunk in range(CHUNKS):
            for way in range(2):
                @pl.when(arrives(way, hop))
                def _():
                    block = origin(way, hop)
                    along(way, hop, chunk, block).wait_recv()
                    if hop + 1 < length - 1:
                        @pl.when(can_send(way, hop + 1))
                        def _():
                            along(way, hop + 1, chunk, block).start()
                    across(way, hop + 1, chunk, block).start()
        for way in range(2):
            @pl.when(arrives(way, hop))
            def _():
                project(origin(way, hop))
        if hop == 0:
            for chunk in range(CHUNKS):
                across(0, 0, chunk, partner).wait_recv()
            project(partner)
    for copy in small[1::2]:
        copy.start()
    for hop in range(1, length):
        for way in range(2):
            @pl.when(arrives(way, hop - 1))
            def _():
                block = origin(way, hop - 1) + partner - me
                for chunk in range(CHUNKS):
                    across(way, hop, chunk, block).wait_recv()
                project(block)
    own_grads.wait()
    own_docs.wait()
    for copy in small:
        copy.wait()

    numbers = docs_s[...]
    counts = [
        jnp.sum(
            jnp.sum(jnp.where(numbers == d, 1.0, 0.0), axis=0), axis=-1, keepdims=True
        )
        for d in range(DOCS - 1)
    ]

    def pick(weight_of, block_of, width):
        total = None
        for b in range(n):
            weight = jnp.concatenate([weight_of(b).astype(jnp.bfloat16)] * (width // HEAD), axis=1)
            term = weight * block_of(b)
            total = term if total is None else total + term
        return total

    numbers = numbers.astype(jnp.float32)
    lane = lax.broadcasted_iota(jnp.int32, (1, BLOCK), 1).astype(jnp.float32)
    pos = lax.broadcasted_iota(jnp.int32, (n * BLOCK, 2 * BLOCK), 0)
    firsts, lasts = [], []
    for b in range(n):
        start = jnp.zeros((1, BLOCK), jnp.float32)
        for d in range(DOCS - 1):
            start = start + jnp.where(numbers[b] > d, counts[d], 0.0)
        firsts.append(start)
        lasts.append(lane + b * BLOCK)

    def packed_row(slot, rows):
        total = jnp.zeros((1, BLOCK), jnp.float32)
        for b in range(n):
            total = total + chosen[slot * n + b] * rows[b]
        return total.astype(jnp.int32)

    def packed_queries(slot):
        return pick(
            lambda b: chosen[slot * n + b], lambda b: q_s[b * BLOCK : (b + 1) * BLOCK, :], HEAD
        )

    def early(it, e, dest):
        return remote(
            g_send.at[0, dest], g_all.at[0, me],
            gs.at[0, 2 * it + e], gr.at[0, 2 * it + (side if it < length - 1 else 0)], seq=dest,
        )

    def early_landed(it, e):
        return remote(
            g_send.at[0, partner], g_all.at[0, partner],
            gs.at[0, 2 * it + e], gr.at[0, 2 * it + e], seq=partner,
        )

    keys, sent_q, landed_q = k_s[...], [], []
    for it in range(length):
        pair = lax.rem(place + 1 + it, length)
        slots = (2 * pair, 2 * pair + 1)
        here = pl.ds(pl.multiple_of(pair * 2 * BLOCK, 2 * BLOCK), 2 * BLOCK)
        first = jnp.concatenate([packed_row(slot, firsts) for slot in slots], axis=1)
        last = jnp.concatenate([packed_row(slot, lasts) for slot in slots], axis=1)
        q = jnp.concatenate([packed_queries(slot) for slot in slots], axis=0)
        packed_s[here, :] = q
        g = grads_s[pl.ds(2 * pair, 2)].reshape(2 * BLOCK, HEAD)
        scores = lax.dot_general(keys, q, NT, preferred_element_type=jnp.float32)
        expon = jnp.where(
            (pos >= first) & (pos <= last),
            jnp.exp2(scores * (FACTOR * math.log2(math.e))),
            0.0,
        )
        prob = expon * (1.0 / jnp.sum(expon, axis=0, keepdims=True))
        prob_low = prob.astype(jnp.bfloat16)
        grad_prob = lax.dot_general(v_s[...], g, NT, preferred_element_type=jnp.float32)
        delta = jnp.sum(prob_low.astype(jnp.float32) * grad_prob, axis=0, keepdims=True)
        dscore = (prob * (grad_prob - delta)).astype(jnp.bfloat16)
        prob_s[:, here] = prob_low
        dscore_s[:, here] = dscore
        dq = lax.dot_general(dscore, keys, TN, preferred_element_type=jnp.float32)
        g_send[0, pl.ds(2 * pair, 2)] = (
            (dq * FACTOR).astype(jnp.bfloat16).reshape(2, BLOCK, HEAD)
        )
        if it < length - 1:
            copies = [early(it, e, slots[e]) for e in range(2)]
            landed_q.extend(early_landed(it, e) for e in range(2))
        else:
            copies = [early(it, 0, partner)]
            landed_q.append(early_landed(it, 0))
        for copy in copies:
            copy.start()
        sent_q.extend(copies)

    def key_sums(p, kept, other, factor):
        total = jnp.dot(kept[...], other, preferred_element_type=jnp.float32)
        g_s[p] = (total * factor).astype(jnp.bfloat16)

    def stage(p):
        for r in range(n):
            g_send[p, r] = pick(
                lambda b: chosen[r * n + b], lambda b: g_s[p, b * BLOCK : (b + 1) * BLOCK, :], HEAD
            )

    def halve(p, b, held):
        size, halved = sizes[b]
        other = pl.multiple_of((1 - bits[b]) * size, size) if halved else 0
        send = remote(
            held.at[p, :, pl.ds(other, size), :], landed[b].at[p], ws.at[b, p], wr.at[b, p],
            dp=partners[b],
        )
        send.start()
        return send

    def weight_part(p):
        w_part[p] = (
            jnp.dot(normed_s[...], g_s[p], preferred_element_type=jnp.float32)
            .astype(jnp.bfloat16)
            .reshape(w_part.shape[1:])
        )
        return halve(p, 0, w_part)

    def grad_copies(p):
        own_g[p].start()
        return [
            remote(
                g_send.at[p, peer], g_all.at[p, me], gs.at[p, k], gr.at[p, k], seq=peer
            )
            for k, peer in enumerate(peers)
        ]

    own_g = [
        pltpu.make_async_copy(g_send.at[p, me], g_all.at[p, me], own_sem.at[4 + p]) for p in range(3)
    ]
    sent_g, halves = [[]], []
    for p in range(3):
        if p == 0:
            own_g[0].start()
            for b in range(n):
                g_s[0, b * BLOCK : (b + 1) * BLOCK, :] = pick(
                    lambda r: chosen[r * n + b], lambda r: g_send[0, r], HEAD
                )
        else:
            if p == 1:
                key_sums(1, dscore_s, packed_s[...], FACTOR)
            else:
                key_sums(2, prob_s, grads_s[...].reshape(n * BLOCK, HEAD), 1.0)
            stage(p)
            sent_g.append(grad_copies(p))
        if p == 1:
            for copy in sent_g[p]:
                copy.start()
        halves.append(weight_part(p))

    held, offset = w_part, 0
    for b, (size, halved) in enumerate(sizes):
        mine = pl.multiple_of(bits[b] * size, size) if halved else 0
        later = []
        for p in range(3):
            halves[p].wait_recv()
            sums[b][p] = (
                held[p, :, pl.ds(mine, size), :].astype(jnp.float32)
                + landed[b][p].astype(jnp.float32)
            ).astype(jnp.bfloat16)
            if b + 1 < count:
                later.append(halve(p, b + 1, sums[b]))
            halves[p].wait_send()
        halves, held, offset = later, sums[b], offset + mine
    size = sizes[-1][0]
    here = pl.ds(pl.multiple_of(offset, size), size)
    sent_w, own_w = [], []
    for p in range(3):
        own = pltpu.make_async_copy(held.at[p, me], w_all.at[p, me, here, :], own_sem.at[7 + p])
        own.start()
        own_w.append(own)
        sent_w.append([
            remote(
                held.at[p, peer], w_all.at[p, me, here, :], ps.at[p, k], pr.at[p, k], seq=peer
            )
            for k, peer in enumerate(peers)
        ])
        for copy in sent_w[p]:
            copy.start()
    for copy in sent_g[2]:
        copy.start()

    def d_part(j):
        columns = jnp.concatenate(
            [g_all[j, h] for h in range(HEADS)], axis=1
        )
        return lax.dot_general(
            columns, weights_s[:, j * HEADS * HEAD : (j + 1) * HEADS * HEAD], NT,
            preferred_element_type=jnp.float32,
        )

    for copy in landed_q:
        copy.wait_recv()
    for copy in sent_q:
        copy.wait_send()
    for p in range(2):
        for copy in [own_g[p]] + sent_g[p]:
            copy.wait()
    d_s[...] = d_part(0) + d_part(1)
    inverse, unit, _ = normalized(
        pick(lambda b: chosen[me * n + b], lambda b: frames_s[b], frames_s.shape[2]), gain[...]
    )

    def d_input():
        for copy in [own_g[2]] + sent_g[2]:
            copy.wait()
        gained = (d_s[...] + d_part(2)) * gain[...]
        mean = jnp.mean(gained * unit, axis=-1, keepdims=True)
        d_out[...] = (inverse * (gained - unit * mean)).astype(jnp.bfloat16)

    spread = [b for b in reversed(range(count)) if sizes[b][1]]

    def widen(p, b, offset):
        size = sizes[b][0]
        here = pl.ds(pl.multiple_of(offset, size), size)
        copy = remote(
            w_all.at[p, :, here, :], w_all.at[p, :, here, :], bs.at[b, p], br.at[b, p],
            dp=partners[b],
        )
        copy.start()
        return copy

    spreading = []
    for p in range(3):
        for copy in [own_w[p]] + sent_w[p]:
            copy.wait()
        if spread:
            spreading.append(widen(p, spread[0], offset))
    for place_of, b in enumerate(spread):
        offset = offset - bits[b] * sizes[b][0]
        later = []
        for p in range(3):
            spreading[p].wait()
            if place_of + 1 < len(spread):
                later.append(widen(p, spread[place_of + 1], offset))
        spreading = later
        if place_of + 2 == len(spread):
            d_input()
    if len(spread) < 2:
        d_input()

    for chunk in range(CHUNKS):
        across(0, 0, chunk, me).wait_send()
        for way in range(2):
            for hop in range(length - 1):
                @pl.when(can_send(way, hop))
                def _():
                    along(way, hop, chunk, me).wait_send()

                @pl.when(arrives(way, hop))
                def _():
                    across(way, hop + 1, chunk, me).wait_send()


def results_kernel(scale, d_in, w_in, d_out, w_out):
    d_out[0] = d_in[...]
    for h in range(HEADS):
        w_out[:, h * HEAD : (h + 1) * HEAD] = w_in[0, h].astype(jnp.float32) * scale


def results(scale, d_frames, w_all):
    rows, width = d_frames.shape
    _, n, w_rows, _ = w_all.shape
    return pl.pallas_call(
        functools.partial(results_kernel, scale),
        grid=(3,),
        in_specs=[
            pl.BlockSpec((rows, width), lambda j: (0, 0)),
            pl.BlockSpec((1, n, w_rows, HEAD), lambda j: (j, 0, 0, 0)),
        ],
        out_specs=(
            pl.BlockSpec((1, rows, width), lambda j: (0, 0, 0)),
            pl.BlockSpec((w_rows, HEADS * HEAD), lambda j: (0, j)),
        ),
        out_shape=(
            jax.ShapeDtypeStruct((1, rows, width), jnp.bfloat16),
            jax.ShapeDtypeStruct((w_rows, 3 * HEADS * HEAD), jnp.float32),
        ),
        name="results",
    )(d_frames, w_all)


def body(n, groups, layer_rows, doc_ids, packing, norm_gain, w_qkv, d_attn):
    width = w_qkv.shape[0]
    total = n * BLOCK
    rows = width // n
    sizes = halvings(rows, groups)
    count = len(sizes)
    dma = pltpu.SemaphoreType.DMA
    low = jnp.bfloat16
    hbm = pl.BlockSpec(memory_space=pl.ANY)
    vmem = pl.BlockSpec(memory_space=pltpu.VMEM)
    buffers = [pltpu.VMEM((3, n, size, HEAD), low) for size, _ in sizes]
    routes = dma((2, n // 2, CHUNKS))
    d_frames, w_all = pl.pallas_call(
        functools.partial(kernel, n, groups),
        out_shape=(
            jax.ShapeDtypeStruct((BLOCK, width), low),
            jax.ShapeDtypeStruct((3, n, rows, HEAD), low),
        ),
        in_specs=[vmem, hbm, vmem, hbm, hbm, hbm],
        out_specs=(vmem, hbm),
        scratch_shapes=[
            pltpu.VMEM((n, BLOCK, width), low),
            pltpu.VMEM((n, 1, BLOCK), jnp.int32),
            pltpu.VMEM((n, BLOCK, HEAD), low),
            pltpu.VMEM(w_qkv.shape, low),
            pltpu.VMEM((width, total), low),
            pltpu.VMEM((total, HEAD), low),
            pltpu.VMEM((total, HEAD), low),
            pltpu.VMEM((total, HEAD), low),
            pltpu.VMEM((total, total), low),
            pltpu.VMEM((total, total), low),
            pltpu.VMEM((total, HEAD), low),
            pltpu.VMEM((3, total, HEAD), low),
            pltpu.VMEM((3, n, BLOCK, HEAD), low),
            pltpu.VMEM((3, n, BLOCK, HEAD), low),
            pltpu.VMEM((3, n, rows, HEAD), low),
            pltpu.VMEM((n * n, 1, HEAD), jnp.float32),
            pltpu.VMEM((BLOCK, width), jnp.float32),
            dma((10,)),
            *buffers, *buffers,
            routes, routes, routes, routes,
            dma((n,)), dma((n,)), dma((n,)), dma((n,)), dma((3, n)), dma((3, n)),
            dma((count, 3)), dma((count, 3)), dma((3, n)), dma((3, n)), dma((count, 3)), dma((count, 3)),
        ],
        compiler_params=pltpu.CompilerParams(
            collective_id=0, has_side_effects=True, vmem_limit_bytes=VMEM_LIMIT
        ),
        name="attention_backward",
    )(packing, layer_rows[0], norm_gain.reshape(1, -1), w_qkv, doc_ids, d_attn[0])
    return results(1.0 / math.sqrt(total * groups), d_frames, w_all)


def solution(mesh):
    return jax.shard_map(
        functools.partial(body, mesh.shape["seq"], mesh.shape["dp"]),
        mesh=mesh,
        in_specs=(
            P("dp", "seq", None),
            P("dp", "seq"),
            P("dp", None),
            P(),
            P(),
            P("dp", "seq", None),
        ),
        out_specs=(P("dp", "seq", None), P("seq", None)),
        check_vma=False,
    )
```

```python
import functools
import math

import jax
import jax.numpy as jnp
from jax import lax
from jax.experimental import pallas as pl
from jax.experimental.pallas import tpu as pltpu
from jax.sharding import PartitionSpec as P

HEADS = 8
HEAD = 128
BLOCK = 128
DOCS = 6
EPS = 1e-05
FACTOR = 1.0 / math.sqrt(HEAD)
MESH = pl.DeviceIdType.MESH
VMEM_LIMIT = 56 * 1024 * 1024
CHUNKS = 2
NT = (((1,), (1,)), ((), ()))
TN = (((0,), (0,)), ((), ()))


def remote(src, dst, send, recv, **where):
    return pltpu.make_async_remote_copy(
        src_ref=src, dst_ref=dst, send_sem=send, recv_sem=recv, device_id=where, device_id_type=MESH
    )


def normalized(frames, gain):
    values = frames.astype(jnp.float32)
    inverse = lax.rsqrt(jnp.mean(values * values, axis=-1, keepdims=True) + EPS)
    unit = values * inverse
    return inverse, unit, (unit * gain).astype(jnp.bfloat16)


def halvings(rows, groups):
    sizes = []
    for _ in range(groups.bit_length() - 1):
        halved = rows % 32 == 0
        rows = rows // 2 if halved else rows
        sizes.append((rows, halved))
    return sizes


def kernel(
    n, groups, packing, frames, gain, w_qkv, docs, grads, d_out, w_all,
    frames_s, docs_s, grads_s, weights_s, normed_s, q_s, k_s, v_s, prob_s, dscore_s,
    packed_s, g_s, g_send, g_all, w_part, chosen, d_s, own_sem, *scratch,
):
    sizes = halvings(w_part.shape[2], groups)
    count = len(sizes)
    landed, sums = scratch[:count], scratch[count : 2 * count]
    zs, zr, ys, yr, ds, dr, ts, tr, gs, gr, ws, wr, ps, pr, bs, br = scratch[2 * count :]
    me = lax.axis_index("seq")
    dp = lax.axis_index("dp")
    side = lax.rem(me, 2)
    place = me // 2
    partner = me + 1 - 2 * side
    length = n // 2
    part = BLOCK // CHUNKS
    head = lax.rem(me, HEADS)
    peers = [lax.rem(me + k, n) for k in range(1, n)]
    bits = [lax.rem(dp // (1 << b), 2) for b in range(count)]
    partners = [dp + (1 << b) * (1 - 2 * bits[b]) for b in range(count)]

    def head_of(device):
        start = pl.multiple_of(lax.rem(device, HEADS) * HEAD, HEAD)
        return grads.at[:, pl.ds(start, HEAD)]

    barrier = pltpu.get_barrier_semaphore()
    for peer in peers:
        pl.semaphore_signal(barrier, inc=1, device_id={"seq": peer}, device_id_type=MESH)
    for other in partners:
        pl.semaphore_signal(barrier, inc=1, device_id={"dp": other}, device_id_type=MESH)
    own_frames = pltpu.make_async_copy(frames, frames_s.at[me], own_sem.at[0])
    own_weights = pltpu.make_async_copy(w_qkv, weights_s, own_sem.at[1])
    own_grads = pltpu.make_async_copy(head_of(me), grads_s.at[me], own_sem.at[2])
    own_docs = pltpu.make_async_copy(docs, docs_s.at[me], own_sem.at[3])
    for copy in (own_frames, own_weights, own_grads, own_docs):
        copy.start()
    pl.semaphore_wait(barrier, n - 1 + count)

    def piece(block, chunk):
        return frames_s.at[block, pl.ds(chunk * part, part), :]

    def along(way, hop, chunk, block, source=None):
        return remote(
            piece(block, chunk) if source is None else source, piece(block, chunk),
            zs.at[way, hop, chunk], zr.at[way, hop, chunk], seq=me + (2 if way == 0 else -2),
        )

    def across(way, hop, chunk, block, source=None):
        return remote(
            piece(block, chunk) if source is None else source, piece(block, chunk),
            ys.at[way, hop, chunk], yr.at[way, hop, chunk], seq=partner,
        )

    def can_send(way, hop):
        if way == 0:
            return (place + 1 < length) & (place - hop >= 0)
        return (place - 1 >= 0) & (place + hop < length)

    def arrives(way, hop):
        return place - 1 - hop >= 0 if way == 0 else place + 1 + hop < length

    def origin(way, hop):
        return me - 2 * (hop + 1) if way == 0 else me + 2 * (hop + 1)

    for chunk in range(CHUNKS):
        source = frames.at[pl.ds(chunk * part, part), :]
        for way in range(2):
            @pl.when(can_send(way, 0))
            def _():
                along(way, 0, chunk, me, source).start()
        across(0, 0, chunk, me, source).start()
    small = []
    for k in range(1, n):
        small.append(remote(docs, docs_s.at[me], ds.at[k - 1], dr.at[k - 1], seq=peers[k - 1]))
        small.append(
            remote(head_of(peers[k - 1]), grads_s.at[me], ts.at[k - 1], tr.at[k - 1], seq=peers[k - 1])
        )
    for copy in small[::2]:
        copy.start()

    def project(block):
        rows = pl.ds(pl.multiple_of(block * BLOCK, BLOCK), BLOCK)
        normed = normalized(frames_s[block], gain[...])[2]
        normed_s[:, rows] = normed.T
        for j, kept in enumerate((q_s, k_s, v_s)):
            columns = pl.ds(pl.multiple_of((j * HEADS + head) * HEAD, HEAD), HEAD)
            kept[rows, :] = jnp.dot(
                normed, weights_s[:, columns], preferred_element_type=jnp.float32
            ).astype(jnp.bfloat16)

    order = packing[...]
    for r in range(n):
        for b in range(n):
            chosen[r * n + b] = jnp.broadcast_to(
                jnp.where(order[:, r : r + 1] == b, 1.0, 0.0), (1, HEAD)
            )
    own_frames.wait()
    own_weights.wait()
    project(me)
    for hop in range(length - 1):
        for chunk in range(CHUNKS):
            for way in range(2):
                @pl.when(arrives(way, hop))
                def _():
                    block = origin(way, hop)
                    along(way, hop, chunk, block).wait_recv()
                    if hop + 1 < length - 1:
                        @pl.when(can_send(way, hop + 1))
                        def _():
                            along(way, hop + 1, chunk, block).start()
                    across(way, hop + 1, chunk, block).start()
        for way in range(2):
            @pl.when(arrives(way, hop))
            def _():
                project(origin(way, hop))
        if hop == 0:
            for chunk in range(CHUNKS):
                across(0, 0, chunk, partner).wait_recv()
            project(partner)
    for copy in small[1::2]:
        copy.start()
    for hop in range(1, length):
        for way in range(2):
            @pl.when(arrives(way, hop - 1))
            def _():
                block = origin(way, hop - 1) + partner - me
                for chunk in range(CHUNKS):
                    across(way, hop, chunk, block).wait_recv()
                project(block)
    own_grads.wait()
    own_docs.wait()
    for copy in small:
        copy.wait()

    numbers = docs_s[...]
    counts = [
        jnp.sum(
            jnp.sum(jnp.where(numbers == d, 1.0, 0.0), axis=0), axis=-1, keepdims=True
        )
        for d in range(DOCS - 1)
    ]

    def first_of(block):
        own = docs_s[block]
        start = jnp.zeros(own.shape, jnp.float32)
        for d in range(DOCS - 1):
            start = start + jnp.where(own > d, counts[d], 0.0)
        return start.astype(jnp.int32)

    def pick(weight_of, block_of, width):
        total = None
        for b in range(n):
            weight = jnp.concatenate([weight_of(b).astype(jnp.bfloat16)] * (width // HEAD), axis=1)
            term = weight * block_of(b)
            total = term if total is None else total + term
        return total

    def grads_of(block):
        return pick(lambda r: chosen[r * n + block], lambda r: grads_s[r], HEAD)

    for i in range(n // 2):
        low, high = 2 * i * BLOCK, 2 * (i + 1) * BLOCK
        first = jnp.concatenate([first_of(2 * i), first_of(2 * i + 1)], axis=1)
        last = low + lax.broadcasted_iota(jnp.int32, (1, 2 * BLOCK), 1)
        pos = lax.broadcasted_iota(jnp.int32, (high, 2 * BLOCK), 0)
        q = q_s[low:high, :]
        g = jnp.concatenate([grads_of(2 * i), grads_of(2 * i + 1)], axis=0)
        packed_s[low:high, :] = g
        keys = k_s[:high, :]
        scores = lax.dot_general(keys, q, NT, preferred_element_type=jnp.float32)
        expon = jnp.where(
            (pos >= first) & (pos <= last),
            jnp.exp2(scores * (FACTOR * math.log2(math.e))),
            0.0,
        )
        prob = expon * (1.0 / jnp.sum(expon, axis=0, keepdims=True))
        prob_low = prob.astype(jnp.bfloat16)
        grad_prob = lax.dot_general(v_s[:high, :], g, NT, preferred_element_type=jnp.float32)
        delta = jnp.sum(prob_low.astype(jnp.float32) * grad_prob, axis=0, keepdims=True)
        dscore = (prob * (grad_prob - delta)).astype(jnp.bfloat16)
        prob_s[:high, low:high] = prob_low
        dscore_s[:high, low:high] = dscore
        dq = lax.dot_general(dscore, keys, TN, preferred_element_type=jnp.float32)
        g_s[0, low:high, :] = (dq * FACTOR).astype(jnp.bfloat16)

    def key_sums(p, kept, other_of, factor):
        for j in range(n // 2):
            low, high = 2 * j * BLOCK, 2 * (j + 1) * BLOCK
            total = jnp.dot(
                kept[low:high, low:], other_of(low), preferred_element_type=jnp.float32
            )
            g_s[p, low:high, :] = (total * factor).astype(jnp.bfloat16)

    def stage(p):
        for r in range(n):
            g_send[p, r] = pick(
                lambda b: chosen[r * n + b], lambda b: g_s[p, b * BLOCK : (b + 1) * BLOCK, :], HEAD
            )

    def halve(p, b, held):
        size, halved = sizes[b]
        other = pl.multiple_of((1 - bits[b]) * size, size) if halved else 0
        send = remote(
            held.at[p, :, pl.ds(other, size), :], landed[b].at[p], ws.at[b, p], wr.at[b, p],
            dp=partners[b],
        )
        send.start()
        return send

    def weight_part(p):
        w_part[p] = (
            jnp.dot(normed_s[...], g_s[p], preferred_element_type=jnp.float32)
            .astype(jnp.bfloat16)
            .reshape(w_part.shape[1:])
        )
        return halve(p, 0, w_part)

    def grad_copies(p):
        own_g[p].start()
        return [
            remote(
                g_send.at[p, peer], g_all.at[p, me], gs.at[p, k], gr.at[p, k], seq=peer
            )
            for k, peer in enumerate(peers)
        ]

    own_g = [
        pltpu.make_async_copy(g_send.at[p, me], g_all.at[p, me], own_sem.at[4 + p]) for p in range(3)
    ]
    sent_g, halves = [], []
    for p in range(3):
        if p == 1:
            key_sums(1, dscore_s, lambda low: q_s[low:, :], FACTOR)
        if p == 2:
            key_sums(2, prob_s, lambda low: packed_s[low:, :], 1.0)
        stage(p)
        sent_g.append(grad_copies(p))
        if p < 2:
            for copy in sent_g[p]:
                copy.start()
        halves.append(weight_part(p))

    held, offset = w_part, 0
    for b, (size, halved) in enumerate(sizes):
        mine = pl.multiple_of(bits[b] * size, size) if halved else 0
        later = []
        for p in range(3):
            halves[p].wait_recv()
            sums[b][p] = (
                held[p, :, pl.ds(mine, size), :].astype(jnp.float32)
                + landed[b][p].astype(jnp.float32)
            ).astype(jnp.bfloat16)
            if b + 1 < count:
                later.append(halve(p, b + 1, sums[b]))
            halves[p].wait_send()
        halves, held, offset = later, sums[b], offset + mine
    size = sizes[-1][0]
    here = pl.ds(pl.multiple_of(offset, size), size)
    sent_w, own_w = [], []
    for p in range(3):
        own = pltpu.make_async_copy(held.at[p, me], w_all.at[p, me, here, :], own_sem.at[7 + p])
        own.start()
        own_w.append(own)
        sent_w.append([
            remote(
                held.at[p, peer], w_all.at[p, me, here, :], ps.at[p, k], pr.at[p, k], seq=peer
            )
            for k, peer in enumerate(peers)
        ])
        for copy in sent_w[p]:
            copy.start()
    for copy in sent_g[2]:
        copy.start()

    def d_part(j):
        columns = jnp.concatenate(
            [g_all[j, h] for h in range(HEADS)], axis=1
        )
        return lax.dot_general(
            columns, weights_s[:, j * HEADS * HEAD : (j + 1) * HEADS * HEAD], NT,
            preferred_element_type=jnp.float32,
        )

    for p in range(2):
        for copy in [own_g[p]] + sent_g[p]:
            copy.wait()
    d_s[...] = d_part(0) + d_part(1)
    inverse, unit, _ = normalized(
        pick(lambda b: chosen[me * n + b], lambda b: frames_s[b], frames_s.shape[2]), gain[...]
    )

    def d_input():
        for copy in [own_g[2]] + sent_g[2]:
            copy.wait()
        gained = (d_s[...] + d_part(2)) * gain[...]
        mean = jnp.mean(gained * unit, axis=-1, keepdims=True)
        d_out[...] = (inverse * (gained - unit * mean)).astype(jnp.bfloat16)

    spread = [b for b in reversed(range(count)) if sizes[b][1]]

    def widen(p, b, offset):
        size = sizes[b][0]
        here = pl.ds(pl.multiple_of(offset, size), size)
        copy = remote(
            w_all.at[p, :, here, :], w_all.at[p, :, here, :], bs.at[b, p], br.at[b, p],
            dp=partners[b],
        )
        copy.start()
        return copy

    spreading = []
    for p in range(3):
        for copy in [own_w[p]] + sent_w[p]:
            copy.wait()
        if spread:
            spreading.append(widen(p, spread[0], offset))
    for place_of, b in enumerate(spread):
        offset = offset - bits[b] * sizes[b][0]
        later = []
        for p in range(3):
            spreading[p].wait()
            if place_of + 1 < len(spread):
                later.append(widen(p, spread[place_of + 1], offset))
        spreading = later
        if place_of + 2 == len(spread):
            d_input()
    if len(spread) < 2:
        d_input()

    for chunk in range(CHUNKS):
        across(0, 0, chunk, me).wait_send()
        for way in range(2):
            for hop in range(length - 1):
                @pl.when(can_send(way, hop))
                def _():
                    along(way, hop, chunk, me).wait_send()

                @pl.when(arrives(way, hop))
                def _():
                    across(way, hop + 1, chunk, me).wait_send()


def results_kernel(scale, d_in, w_in, d_out, w_out):
    d_out[0] = d_in[...]
    for h in range(HEADS):
        w_out[:, h * HEAD : (h + 1) * HEAD] = w_in[0, h].astype(jnp.float32) * scale


def results(scale, d_frames, w_all):
    rows, width = d_frames.shape
    _, n, w_rows, _ = w_all.shape
    return pl.pallas_call(
        functools.partial(results_kernel, scale),
        grid=(3,),
        in_specs=[
            pl.BlockSpec((rows, width), lambda j: (0, 0)),
            pl.BlockSpec((1, n, w_rows, HEAD), lambda j: (j, 0, 0, 0)),
        ],
        out_specs=(
            pl.BlockSpec((1, rows, width), lambda j: (0, 0, 0)),
            pl.BlockSpec((w_rows, HEADS * HEAD), lambda j: (0, j)),
        ),
        out_shape=(
            jax.ShapeDtypeStruct((1, rows, width), jnp.bfloat16),
            jax.ShapeDtypeStruct((w_rows, 3 * HEADS * HEAD), jnp.float32),
        ),
        name="results",
    )(d_frames, w_all)


def body(n, groups, layer_rows, doc_ids, packing, norm_gain, w_qkv, d_attn):
    width = w_qkv.shape[0]
    total = n * BLOCK
    rows = width // n
    sizes = halvings(rows, groups)
    count = len(sizes)
    dma = pltpu.SemaphoreType.DMA
    low = jnp.bfloat16
    hbm = pl.BlockSpec(memory_space=pl.ANY)
    vmem = pl.BlockSpec(memory_space=pltpu.VMEM)
    buffers = [pltpu.VMEM((3, n, size, HEAD), low) for size, _ in sizes]
    routes = dma((2, n // 2, CHUNKS))
    d_frames, w_all = pl.pallas_call(
        functools.partial(kernel, n, groups),
        out_shape=(
            jax.ShapeDtypeStruct((BLOCK, width), low),
            jax.ShapeDtypeStruct((3, n, rows, HEAD), low),
        ),
        in_specs=[vmem, hbm, vmem, hbm, hbm, hbm],
        out_specs=(vmem, hbm),
        scratch_shapes=[
            pltpu.VMEM((n, BLOCK, width), low),
            pltpu.VMEM((n, 1, BLOCK), jnp.int32),
            pltpu.VMEM((n, BLOCK, HEAD), low),
            pltpu.VMEM(w_qkv.shape, low),
            pltpu.VMEM((width, total), low),
            pltpu.VMEM((total, HEAD), low),
            pltpu.VMEM((total, HEAD), low),
            pltpu.VMEM((total, HEAD), low),
            pltpu.VMEM((total, total), low),
            pltpu.VMEM((total, total), low),
            pltpu.VMEM((total, HEAD), low),
            pltpu.VMEM((3, total, HEAD), low),
            pltpu.VMEM((3, n, BLOCK, HEAD), low),
            pltpu.VMEM((3, n, BLOCK, HEAD), low),
            pltpu.VMEM((3, n, rows, HEAD), low),
            pltpu.VMEM((n * n, 1, HEAD), jnp.float32),
            pltpu.VMEM((BLOCK, width), jnp.float32),
            dma((10,)),
            *buffers, *buffers,
            routes, routes, routes, routes,
            dma((n,)), dma((n,)), dma((n,)), dma((n,)), dma((3, n)), dma((3, n)),
            dma((count, 3)), dma((count, 3)), dma((3, n)), dma((3, n)), dma((count, 3)), dma((count, 3)),
        ],
        compiler_params=pltpu.CompilerParams(
            collective_id=0, has_side_effects=True, vmem_limit_bytes=VMEM_LIMIT
        ),
        name="attention_backward",
    )(packing, layer_rows[0], norm_gain.reshape(1, -1), w_qkv, doc_ids, d_attn[0])
    return results(1.0 / math.sqrt(total * groups), d_frames, w_all)


def solution(mesh):
    return jax.shard_map(
        functools.partial(body, mesh.shape["seq"], mesh.shape["dp"]),
        mesh=mesh,
        in_specs=(
            P("dp", "seq", None),
            P("dp", "seq"),
            P("dp", None),
            P(),
            P(),
            P("dp", "seq", None),
        ),
        out_specs=(P("dp", "seq", None), P("seq", None)),
        check_vma=False,
    )
```
